32 devices in a mesh: section: 2 (over core), dp: 4 (over z), tensor: 4 (over y, x).
Axes of the slice: x: 2, y: 2, z: 4, core: 2. Of those that a mesh axis runs over, the one named last changes fastest.
Arguments:
- inputs: bfloat16 [4, 2, 256, 768], P('dp', None, 'tensor'), may hold values from -6 to 6
- cotangent: bfloat16 [4, 2, 256, 768], P('dp', None, 'tensor'), may hold values from -6 to 6
- segments: int32 [4, 2, 256], P('dp'), may hold values from 0 to 31, never falling along the last dimension, each value on 1 to 128 neighbouring positions
- row_params: bfloat16 [2, 6, 768], P('section', None, 'dp'), may hold values from 0.5 to 1.5
- qv_bias: bfloat16 [2, 2, 4, 192], P('section', None, 'tensor', 'dp'), may hold values from -3 to 3
- w_qkv: bfloat16 [2, 3, 768, 768], P('section', None, 'dp', 'tensor'), may hold values from -0.21875 to 0.21875
- w_out: bfloat16 [2, 768, 768], P('section', 'tensor', 'dp'), may hold values from -0.4375 to 0.4375
- fc1_bias: bfloat16 [2, 4, 768], P('section', 'tensor', 'dp'), may hold values from -3 to 3
- w_fc1: bfloat16 [2, 768, 3072], P('section', 'dp', 'tensor'), may hold values from -0.4375 to 0.4375
- w_fc2: bfloat16 [2, 3072, 768], P('section', 'tensor', 'dp'), may hold values from -0.21875 to 0.21875
Outputs:
- block_out: bfloat16 [2, 4, 2, 256, 768], P('section', 'dp', None, 'tensor')
- input_grads: float32 [2, 4, 2, 256, 768], P('section', 'dp', None, 'tensor')
- row_params_grad: float32 [2, 6, 768], P('section', None, ('dp', 'tensor'))
- qv_bias_grad: float32 [2, 2, 4, 192], P('section', None, 'tensor', 'dp')
- w_qkv_grad: float32 [2, 3, 768, 768], P('section', None, 'dp', 'tensor')
- w_out_grad: float32 [2, 768, 768], P('section', 'tensor', 'dp')
- fc1_bias_grad: float32 [2, 4, 768], P('section', 'tensor', 'dp')
- w_fc1_grad: float32 [2, 768, 3072], P('section', 'dp', 'tensor')
- w_fc2_grad: float32 [2, 3072, 768], P('section', 'tensor', 'dp')
The draws below stay inside these ranges and needn't reach their ends.
Inputs may be any that keep to these rules, and one draw needn't show every extreme that they name: `segments`: document numbers never fall along a pack; every document spans 1 to 128 tokens and one spans exactly 128.
All inputs are finite; a program needn't handle non-finite values.
Results may differ from the reference program's by a relative error of at most 0.014.
Values may be sent and summed in bfloat16 or wider, within the bound.
No kernel may reach another device: no remote copies, remote signals or barrier semaphores. Data moves between devices by JAX's collectives and lax.ppermute only.
A program may use at most 128 MiB of HBM per device.

```python
import math
import jax
import jax.numpy as jnp
import numpy as np
from jax import lax

D = 768
HEADS = 12
HEAD_DIM = 64
FF = 3072
TOK_MB = 256
MB = 2
SECTIONS = 2
MICRO_PACKS = 4
SPLITS = 4
QV_COLS = 192
FF_COLS = 768
SEG_COUNT = 32
SEG_MOST = 128


def spiked(values, own_key, source, target, parts, factor):
    def block_of(dim):
        return (jnp.arange(values.shape[dim]) // (values.shape[dim] // parts)).reshape((-1,) + (1,) * (values.ndim - 1 - dim))

    first = jax.random.permutation(own_key, parts)[block_of(target)]
    second = (block_of(target) + parts // 2) % parts
    return jnp.where((block_of(source) == first) | (block_of(source) == second), factor * values, values)


def steps_of(own_key, shape, pieces, least, largest):
    level = 1.0
    for dim, shards_of in pieces:
        draws = jax.random.uniform(jax.random.fold_in(jax.random.fold_in(own_key, 6), dim), (shards_of,), jnp.float32, least / len(pieces), largest / len(pieces))
        level = level * jnp.repeat(jnp.exp(draws), shape[dim] // shards_of).reshape((-1,) + (1,) * (len(shape) - 1 - dim))
    return level


def split_up(amount, total, reach, slope):
    loads = [(1 << 20) // math.isqrt(rank ** slope) + 1 for rank in range(2, amount + 1)]
    rest, given = total - reach - (amount - 1), [1] * (amount - 1)
    while rest > 0:
        free = [i for i in range(amount - 1) if given[i] < reach]
        pool, left = sum([loads[i] for i in free]), rest
        for i in free:
            more = min(reach - given[i], max(1, left * loads[i] // pool), rest)
            given[i] = given[i] + more
            rest = rest - more
    return np.array([reach] + given)


def ragged_sizes(own_key, number_of, total, reach, skew):
    if number_of == 2:
        one = jax.random.randint(own_key, (), max(1, total - reach), min(reach, total - 1) + 1)
        return jnp.stack([one, total - one])
    tallies = jnp.asarray(split_up(number_of, total, reach, skew), jnp.int32)
    twos = (number_of - 1) // 2
    donor, taker = tallies[1:1 + 2 * twos:2], tallies[2:2 + 2 * twos:2]
    room = jnp.minimum(donor - 1, reach - taker)
    shifted = jax.random.randint(jax.random.fold_in(own_key, 1), (twos,), 0, 1 << 20) % (room + 1)
    tallies = tallies.at[1:1 + 2 * twos:2].set(donor - shifted).at[2:2 + 2 * twos:2].set(taker + shifted)
    return tallies[jax.random.permutation(jax.random.fold_in(own_key, 2), number_of)]


def gaussian(own_key, shape, spread, bound, split=(), kind=jnp.bfloat16):
    loudness = steps_of(own_key, shape, split, -0.22, 0.18) if split else 1.0
    drawn = jax.random.normal(own_key, shape, jnp.float32) * spread * loudness
    return jnp.minimum(jnp.maximum(drawn, -bound), bound).astype(kind)


def bell_draw_with(rng, dims, deviation, limit, split, heavy, held_as=jnp.bfloat16):
    values = deviation * jax.random.normal(rng, dims, jnp.float32)
    if split:
        values = values * steps_of(rng, dims, split, -0.22, 0.18)
    return jnp.clip(spiked(values, jax.random.fold_in(rng, 3), *heavy), -limit, limit).astype(held_as)


def setup_inputs(seed: int = 0) -> dict:
    streams_of = jax.random.split(jax.random.key(seed), 11)
    inputs = gaussian(streams_of[0], (MICRO_PACKS, MB, TOK_MB, D), 1.0, 6.0, ((0, 4), (2, 4)))
    cotangent = bell_draw_with(streams_of[1], (MICRO_PACKS, MB, TOK_MB, D), 1.0, 6.0, ((0, 4), (2, 4)), (0, 3, 4, 2.0))
    segments = jax.vmap(lambda own: jnp.searchsorted(jnp.cumsum(ragged_sizes(own, SEG_COUNT, TOK_MB, SEG_MOST, 2)), jnp.arange(TOK_MB), side="right"))(jax.random.split(streams_of[2], MICRO_PACKS * MB)).reshape((MICRO_PACKS, MB, TOK_MB)).astype(jnp.int32)
    row_params = jnp.clip(1.0 + 0.1 * jax.random.normal(streams_of[3], (SECTIONS, 6, D), jnp.float32), 0.5, 1.5).astype(jnp.bfloat16)
    qv_bias = gaussian(streams_of[4], (SECTIONS, 2, SPLITS, QV_COLS), 0.5, 3.0, ((0, 2), (2, 4), (3, 4)))
    w_qkv = gaussian(streams_of[5], (SECTIONS, 3, D, D), D ** -0.5, 0.21875, ((0, 2), (2, 4), (3, 4)))
    w_out = gaussian(streams_of[6], (SECTIONS, D, D), (D // 4) ** -0.5, 0.4375, ((0, 2), (1, 4), (2, 4)))
    fc1_bias = gaussian(streams_of[7], (SECTIONS, SPLITS, FF_COLS), 0.5, 3.0, ((0, 2), (1, 4), (2, 4)))
    w_fc1 = gaussian(streams_of[8], (SECTIONS, D, FF), (D // 4) ** -0.5, 0.4375, ((0, 2), (1, 4), (2, 4)))
    w_fc2 = gaussian(streams_of[9], (SECTIONS, FF, D), (FF // 4) ** -0.5, 0.21875, ((0, 2), (1, 4), (2, 4)))
    return {"inputs": inputs, "cotangent": cotangent, "segments": segments, "row_params": row_params, "qv_bias": qv_bias, "w_qkv": w_qkv, "w_out": w_out, "fc1_bias": fc1_bias, "w_fc1": w_fc1, "w_fc2": w_fc2}


EPSILON = 1e-05
NEG_LARGE = -1e+30
GELU_SCALE = 0.7978845608028654
GELU_CUBIC = 0.044715

def norm_rows(values):
    center = values - lax.optimization_barrier(jnp.mean(values, axis=-1, keepdims=True))
    inverse = lax.rsqrt(lax.optimization_barrier(jnp.mean(center * center, axis=-1, keepdims=True)) + EPSILON)
    return (center * inverse, inverse)

def norm_back(grads, normed, inverse, gain):
    scaled = grads * gain
    back = inverse * (scaled - lax.optimization_barrier(jnp.mean(scaled, axis=-1, keepdims=True)) - normed * lax.optimization_barrier(jnp.mean(scaled * normed, axis=-1, keepdims=True)))
    return (back, lax.optimization_barrier(jnp.sum(grads * normed, axis=0)), lax.optimization_barrier(jnp.sum(grads, axis=0)))

def gelu_parts(hidden):
    tangent = jnp.tanh(GELU_SCALE * (hidden + GELU_CUBIC * hidden * hidden * hidden))
    activated = 0.5 * hidden * (1.0 + tangent)
    derivative = 0.5 * (1.0 + tangent) + 0.5 * hidden * (1.0 - tangent * tangent) * GELU_SCALE * (1.0 + 3.0 * GELU_CUBIC * hidden * hidden)
    return (activated, derivative)

def allowed_mask(segment_ids):
    position = jnp.arange(segment_ids.shape[0], dtype=jnp.int32)
    flags = (segment_ids[:, None] == segment_ids[None, :]) & (position[None, :] <= position[:, None])
    return flags.astype(jnp.int32)

def scores_of(queries, keys_all, allowed):
    raw = jnp.einsum('qhd,khd->hqk', queries.astype(jnp.float32), keys_all.astype(jnp.float32)) / math.sqrt(HEAD_DIM)
    return jnp.where(allowed[None] == 1, raw, NEG_LARGE)

def layer_forward(stream_in, segment_ids, params):
    row_params, column_bias, proj_qkv, proj_out, hidden_bias, proj_up, proj_down = params
    row_values = row_params.astype(jnp.float32)
    column_bias = column_bias.astype(jnp.float32)
    pack_len = stream_in.shape[0]
    stream = stream_in.astype(jnp.float32)
    normed_one, inverse_one = norm_rows(stream)
    attn_rows = (normed_one * row_values[0] + row_values[1]).astype(jnp.bfloat16)
    queries = (jnp.dot(attn_rows, proj_qkv[0], preferred_element_type=jnp.float32) + column_bias[0]).astype(jnp.bfloat16).reshape(pack_len, HEADS, HEAD_DIM)
    keys_all = jnp.dot(attn_rows, proj_qkv[1], preferred_element_type=jnp.float32).astype(jnp.bfloat16).reshape(pack_len, HEADS, HEAD_DIM)
    values_all = (jnp.dot(attn_rows, proj_qkv[2], preferred_element_type=jnp.float32) + column_bias[1]).astype(jnp.bfloat16).reshape(pack_len, HEADS, HEAD_DIM)
    allowed = allowed_mask(segment_ids)
    scores = scores_of(queries, keys_all, allowed)
    row_maximum = lax.optimization_barrier(jnp.max(scores, axis=-1, keepdims=True))
    log_total = row_maximum + jnp.log(lax.optimization_barrier(jnp.sum(jnp.exp(scores - row_maximum), axis=-1, keepdims=True)))
    weights_soft = jnp.exp(scores - log_total).astype(jnp.bfloat16)
    attended = jnp.einsum('hqk,khd->qhd', weights_soft.astype(jnp.float32), values_all.astype(jnp.float32)).reshape(pack_len, D).astype(jnp.bfloat16)
    middle = stream + jnp.dot(attended, proj_out, preferred_element_type=jnp.float32) + row_values[2]
    normed_two, inverse_two = norm_rows(middle)
    mlp_rows = (normed_two * row_values[3] + row_values[4]).astype(jnp.bfloat16)
    activated, derivative = gelu_parts(jnp.dot(mlp_rows, proj_up, preferred_element_type=jnp.float32) + hidden_bias.astype(jnp.float32))
    activated = activated.astype(jnp.bfloat16)
    result = middle + jnp.dot(activated, proj_down, preferred_element_type=jnp.float32) + row_values[5]
    saved_state = (normed_one, inverse_one, attn_rows, queries, keys_all, values_all, log_total, attended, normed_two, inverse_two, mlp_rows, derivative, activated, allowed)
    return (result, saved_state)

def layer_backward(grad_out, saved_state, params):
    row_params, column_bias, proj_qkv, proj_out, hidden_bias, proj_up, proj_down = params
    row_values = row_params.astype(jnp.float32)
    normed_one, inverse_one, attn_rows, queries, keys_all, values_all, log_total, attended, normed_two, inverse_two, mlp_rows, derivative, activated, allowed = saved_state
    pack_len = grad_out.shape[0]
    grad_low = grad_out.astype(jnp.bfloat16)
    grad_down = jnp.dot(activated.T, grad_low, preferred_element_type=jnp.float32)
    grad_hidden = jnp.dot(grad_low, proj_down.T, preferred_element_type=jnp.float32) * derivative
    hidden_low = grad_hidden.astype(jnp.bfloat16)
    grad_hbias = lax.optimization_barrier(jnp.sum(grad_hidden, axis=0))
    grad_up = jnp.dot(mlp_rows.T, hidden_low, preferred_element_type=jnp.float32)
    grad_mlp_in = jnp.dot(hidden_low, proj_up.T, preferred_element_type=jnp.float32)
    back_two, gain_two, shift_two = norm_back(grad_mlp_in, normed_two, inverse_two, row_values[3])
    grad_middle = grad_out + back_two
    middle_low = grad_middle.astype(jnp.bfloat16)
    grad_proj_out = jnp.dot(attended.T, middle_low, preferred_element_type=jnp.float32)
    grad_attended = jnp.dot(middle_low, proj_out.T, preferred_element_type=jnp.float32).astype(jnp.bfloat16).reshape(pack_len, HEADS, HEAD_DIM)
    probabilities = jnp.exp(scores_of(queries, keys_all, allowed) - log_total)
    probs_low = probabilities.astype(jnp.bfloat16)
    grad_values = jnp.einsum('hqk,qhd->khd', probs_low.astype(jnp.float32), grad_attended.astype(jnp.float32)).reshape(pack_len, D)
    grad_probs = jnp.einsum('qhd,khd->hqk', grad_attended.astype(jnp.float32), values_all.astype(jnp.float32))
    row_delta = lax.optimization_barrier(jnp.sum(probabilities * grad_probs, axis=-1, keepdims=True))
    grad_scores = (probabilities * (grad_probs - row_delta) / math.sqrt(HEAD_DIM)).astype(jnp.bfloat16)
    grad_queries = jnp.einsum('hqk,khd->qhd', grad_scores.astype(jnp.float32), keys_all.astype(jnp.float32)).reshape(pack_len, D)
    grad_keys = jnp.einsum('hqk,qhd->khd', grad_scores.astype(jnp.float32), queries.astype(jnp.float32)).reshape(pack_len, D)
    rounded_grads = (grad_queries.astype(jnp.bfloat16), grad_keys.astype(jnp.bfloat16), grad_values.astype(jnp.bfloat16))
    grad_cbias = jnp.stack([lax.optimization_barrier(jnp.sum(grad_queries, axis=0)), lax.optimization_barrier(jnp.sum(grad_values, axis=0))])
    grad_qkv = jnp.stack([jnp.dot(attn_rows.T, piece, preferred_element_type=jnp.float32) for piece in rounded_grads])
    grad_attn_in = jnp.dot(rounded_grads[0], proj_qkv[0].T, preferred_element_type=jnp.float32)
    grad_attn_in = grad_attn_in + jnp.dot(rounded_grads[1], proj_qkv[1].T, preferred_element_type=jnp.float32)
    grad_attn_in = grad_attn_in + jnp.dot(rounded_grads[2], proj_qkv[2].T, preferred_element_type=jnp.float32)
    back_one, gain_one, shift_one = norm_back(grad_attn_in, normed_one, inverse_one, row_values[0])
    grad_in = grad_middle + back_one
    grad_rowvals = jnp.stack([gain_one, shift_one, lax.optimization_barrier(jnp.sum(grad_middle, axis=0)), gain_two, shift_two, lax.optimization_barrier(jnp.sum(grad_out, axis=0))])
    return (grad_in, (grad_rowvals, grad_cbias, grad_qkv, grad_proj_out, grad_hbias, grad_up, grad_down))

def reference(inputs, cotangent, segments, row_params, qv_bias, w_qkv, w_out, fc1_bias, w_fc1, w_fc2):

    def section_params(index):
        return (row_params[index], qv_bias[index].reshape(2, D), w_qkv[index], w_out[index], fc1_bias[index].reshape(FF), w_fc1[index], w_fc2[index])
    params_first = section_params(0)
    params_second = section_params(1)
    packs = MICRO_PACKS * MB
    flat_inputs = inputs.reshape(packs, TOK_MB, D)
    flat_cot = cotangent.reshape(packs, TOK_MB, D)
    flat_seg = segments.reshape(packs, TOK_MB)
    zeros_init = (jnp.zeros((2, 6, D), jnp.float32), jnp.zeros((2, 2, D), jnp.float32), jnp.zeros((2, 3, D, D), jnp.float32), jnp.zeros((2, D, D), jnp.float32), jnp.zeros((2, FF), jnp.float32), jnp.zeros((2, D, FF), jnp.float32), jnp.zeros((2, FF, D), jnp.float32))

    def one_pack(carry, item):
        pack_in, pack_cot, pack_segment_ids = item
        first_out, first_stash = layer_forward(pack_in, pack_segment_ids, params_first)
        boundary = first_out.astype(jnp.bfloat16)
        second_out, second_stash = layer_forward(boundary, pack_segment_ids, params_second)
        grad_boundary, grads_second = layer_backward(pack_cot.astype(jnp.float32), second_stash, params_second)
        grad_input, grads_first = layer_backward(grad_boundary, first_stash, params_first)
        carry = tuple((running + jnp.stack([earlier, later]) for running, earlier, later in zip(carry, grads_first, grads_second)))
        return (carry, (boundary, second_out.astype(jnp.bfloat16), grad_input, grad_boundary))
    total_sums, (boundaries, finals, grad_inputs, grad_bounds) = lax.scan(one_pack, zeros_init, (flat_inputs, flat_cot, flat_seg))
    block_out = jnp.stack([boundaries, finals]).reshape(2, MICRO_PACKS, MB, TOK_MB, D)
    input_grads = jnp.stack([grad_inputs, grad_bounds]).reshape(2, MICRO_PACKS, MB, TOK_MB, D)
    return (block_out, input_grads, total_sums[0], total_sums[1].reshape(2, 2, SPLITS, QV_COLS), total_sums[2], total_sums[3], total_sums[4].reshape(2, SPLITS, FF_COLS), total_sums[5], total_sums[6])
```

```python
import functools
import math

import jax
import jax.numpy as jnp
from jax import lax
from jax.experimental import pallas as pl
from jax.experimental.pallas import tpu as pltpu
from jax.sharding import PartitionSpec as P

HEAD_DIM = 64
EPSILON = 1e-05
NEG_LARGE = -1e30
GELU_SCALE = 0.7978845608028654
GELU_CUBIC = 0.044715
F32 = jnp.float32
BF16 = jnp.bfloat16
VMEM_LIMIT = 20 * 1024 * 1024


def dot(left, right):
    return jnp.dot(left, right, preferred_element_type=F32)


def dot_t(left, right):
    return lax.dot_general(left, right, (((1,), (1,)), ((), ())), preferred_element_type=F32)


def t_dot(left, right):
    return lax.dot_general(left, right, (((0,), (0,)), ((), ())), preferred_element_type=F32)


def norm_rows(values):
    center = values - jnp.mean(values, axis=-1, keepdims=True)
    inverse = lax.rsqrt(jnp.mean(center * center, axis=-1, keepdims=True) + EPSILON)
    return center * inverse, inverse


def norm_back(grads, normed, inverse, gain):
    scaled = grads * gain
    return inverse * (
        scaled
        - jnp.mean(scaled, axis=-1, keepdims=True)
        - normed * jnp.mean(scaled * normed, axis=-1, keepdims=True)
    )


def rows_of(refs):
    return jnp.concatenate([ref[...] for ref in refs], axis=0)


def store_blocks(outs, values, rows):
    for k, out in enumerate(outs):
        out[...] = values[k * rows : (k + 1) * rows].astype(out.dtype)


def summed(own, others):
    total = own[...]
    for ref in others:
        total = total + ref[...].astype(F32)
    return total


def struct(shape, dtype):
    return jax.ShapeDtypeStruct(shape, dtype)


def kept(shape, dtype):
    return pltpu.HBM(shape, dtype)


def far(array):
    return pltpu.with_memory_space_constraint(array, pltpu.HBM)


def call(body, outs, name, flops, args, specs=None, scratch=(), after=()):
    vmem = pl.BlockSpec(memory_space=pltpu.VMEM)
    specs = specs or [vmem] * len(args)
    if after:
        inner, count, extra = body, len(args), len(after)
        specs = specs + [pl.BlockSpec(memory_space=pl.ANY)] * extra
        args = [*args, *after]

        def body(*refs):
            inner(*refs[:count], *refs[count + extra :])

    nbytes = sum(math.prod(a.shape) * a.dtype.itemsize for a in (*args, *outs))
    return pl.pallas_call(
        body,
        out_shape=tuple(outs),
        in_specs=specs,
        out_specs=(vmem,) * len(outs),
        scratch_shapes=scratch,
        compiler_params=pltpu.CompilerParams(vmem_limit_bytes=VMEM_LIMIT),
        cost_estimate=pl.CostEstimate(flops=flops, bytes_accessed=nbytes, transcendentals=0),
        name=name,
    )(*args)


def attn_load(layer, weights, proj, sems):
    split = proj.shape[1] // 3
    copies = [
        pltpu.make_async_copy(weights.at[layer, :, at], proj.at[:, at], sems.at[i])
        for i, at in enumerate((pl.ds(0, split), pl.ds(split, 2 * split)))
    ]
    for copy in copies:
        copy.start()
    return copies


def mlp_load(weights, proj, sems, order):
    halves, rows = weights.shape[0], weights.shape[3]
    copies = [
        pltpu.make_async_copy(
            weights.at[i, :, g], proj.at[g, :, pl.ds(i * rows, rows), :], sems.at[i, g]
        )
        for g in order
        for i in range(halves)
    ]
    for copy in copies:
        copy.start()
    return copies[:halves], copies[halves:]


def wait_all(copies):
    for copy in copies:
        copy.wait()


def mlp_weight(proj, g):
    return proj[g].reshape(-1, proj.shape[-1])


def attn_fwd_body(n, layer, *refs):
    xs, (params, mask, weights), refs = refs[:n], refs[n : n + 3], refs[n + 3 :]
    (x_out, a_out, oqkv_out, lse_out), partials, (proj, sem) = refs[:4], refs[4:-2], refs[-2:]
    loading = attn_load(layer, weights, proj, sem)
    x = rows_of(xs)
    x_out[...] = x
    normed, _ = norm_rows(x.astype(F32))
    a = (normed * params[0:1] + params[1:2]).astype(BF16)
    a_out[...] = a
    width = proj.shape[1] // 4
    wait_all(loading)
    oqkv = (dot(a, proj[...]) + params[7:8]).astype(BF16)
    allowed = mask[...] > 0.5
    heads, logs = [], []
    for h in range(width // HEAD_DIM):
        q, k, v = (
            oqkv[:, (1 + i) * width + h * HEAD_DIM : (1 + i) * width + (h + 1) * HEAD_DIM]
            for i in range(3)
        )
        scores = jnp.where(allowed, dot_t(q, k) * HEAD_DIM**-0.5, NEG_LARGE)
        top = jnp.max(scores, axis=-1, keepdims=True)
        powers = jnp.exp(scores - top)
        total = jnp.sum(powers, axis=-1, keepdims=True)
        logs.append(top + jnp.log(total))
        heads.append(dot((powers * (1.0 / total)).astype(BF16), v).astype(BF16))
    o = jnp.concatenate(heads, axis=1)
    oqkv_out[...] = jnp.concatenate([o, oqkv[:, width:]], axis=1)
    lse_out[...] = jnp.concatenate(logs, axis=1)
    store_blocks(partials, dot_t(o, proj[:, :width]), xs[0].shape[0])


def middle_body(n, *refs):
    x, own, others, params, h_out, c_out = refs[0], refs[1], refs[2 : n + 1], *refs[n + 1 :]
    h = x[...].astype(F32) + summed(own, others) + params[2:3]
    h_out[...] = h
    normed, _ = norm_rows(h)
    c_out[...] = (normed * params[3:4] + params[4:5]).astype(BF16)


def mlp_fwd_body(n, *refs):
    cs, (params, weights) = refs[:n], refs[n : n + 2]
    c_out, m_out, der_out = refs[n + 2 : n + 5]
    partials, (proj, sems) = refs[n + 5 : -2], refs[-2:]
    first, second = mlp_load(weights, proj, sems, (0, 1))
    c = rows_of(cs)
    c_out[...] = c
    wait_all(first)
    u = dot(c, mlp_weight(proj, 0)) + params[6:7]
    tangent = jnp.tanh(GELU_SCALE * (u + GELU_CUBIC * u * u * u))
    m = (0.5 * u * (1.0 + tangent)).astype(BF16)
    der_out[...] = 0.5 * (1.0 + tangent) + 0.5 * u * (1.0 - tangent * tangent) * GELU_SCALE * (
        1.0 + 3.0 * GELU_CUBIC * u * u
    )
    m_out[...] = m
    wait_all(second)
    store_blocks(partials, dot_t(m, mlp_weight(proj, 1)), cs[0].shape[0])


def end_body(n, *refs):
    h, own, others, params, out = refs[0], refs[1], refs[2 : n + 1], *refs[n + 1 :]
    out[...] = (h[...] + summed(own, others) + params[5:6]).astype(BF16)


def mlp_bwd_body(n, *refs):
    es, (der, weights) = refs[:n], refs[n : n + 2]
    e_out, du_out, sum_out = refs[n + 2 : n + 5]
    partials, (proj, sems) = refs[n + 5 : -2], refs[-2:]
    first, second = mlp_load(weights, proj, sems, (1, 0))
    e = rows_of(es)
    e_out[...] = e
    wait_all(first)
    du = dot(e, mlp_weight(proj, 1)) * der[...]
    du_low = du.astype(BF16)
    du_out[...] = du_low
    sum_out[...] = jnp.sum(du, axis=0, keepdims=True)
    wait_all(second)
    store_blocks(partials, dot_t(du_low, mlp_weight(proj, 0)), es[0].shape[0])


def mlp_grads_body(dp, meta, c, e, du, m, keep, send, full):
    full[0] = t_dot(c[...], du[...])
    full[1] = t_dot(e[...], m[...])
    half = full.shape[1] // dp // 2
    first = meta[0] == 0
    for j in range(dp):
        for g in range(2):
            low, high = (full[g, (2 * j + i) * half : (2 * j + i + 1) * half].astype(BF16) for i in range(2))
            at = slice(g * half, (g + 1) * half)
            keep[j, at] = jnp.where(first, low, high)
            send[j, at] = jnp.where(first, high, low)


def middle_back_body(n, *refs):
    e, h, own, others, params = refs[0], refs[1], refs[2], refs[3 : n + 2], refs[n + 2]
    dh_out, low_out, sums_out = refs[n + 3 :]
    dc = summed(own, others)
    e_values = e[...].astype(F32)
    normed, inverse = norm_rows(h[...])
    dh = e_values + norm_back(dc, normed, inverse, params[3:4])
    dh_out[...] = dh
    low_out[...] = dh.astype(BF16)
    sums_out[...] = jnp.concatenate(
        [jnp.sum(v, axis=0, keepdims=True) for v in (dh, dc * normed, dc, e_values)], axis=0
    )


def attn_bwd_body(n, layer, *refs):
    carried = refs[n + 4 : 2 * n + 3] if layer == 0 else ()
    refs = refs[: n + 4] + refs[n + 4 + len(carried) :]
    dhs, (weights, oqkv_ref, lse, mask) = refs[:n], refs[n : n + 4]
    dh_out, dqkv_out, sums_out = refs[n + 4 : n + 7]
    partials, (proj, sem) = refs[n + 7 : -2], refs[-2:]
    loading = attn_load(layer, weights, proj, sem)
    dh = rows_of(dhs)
    dh_out[...] = dh
    loading[0].wait()
    width = proj.shape[1] // 4
    scale = HEAD_DIM**-0.5
    do = dot(dh, proj[:, :width]).astype(BF16)
    oqkv = oqkv_ref[...]
    allowed = mask[...] > 0.5
    dqs, dks, dvs = [], [], []
    for h in range(width // HEAD_DIM):
        q, k, v = (
            oqkv[:, (1 + i) * width + h * HEAD_DIM : (1 + i) * width + (h + 1) * HEAD_DIM]
            for i in range(3)
        )
        do_h = do[:, h * HEAD_DIM : (h + 1) * HEAD_DIM]
        scores = jnp.where(allowed, dot_t(q, k) * scale, NEG_LARGE)
        probs = jnp.exp(scores - lse[:, h : h + 1])
        dvs.append(t_dot(probs.astype(BF16), do_h))
        dp = dot_t(do_h, v)
        delta = jnp.sum(probs * dp, axis=-1, keepdims=True)
        ds = (probs * (dp - delta) * scale).astype(BF16)
        dqs.append(dot(ds, k))
        dks.append(t_dot(ds, q))
    dq, dk, dv = (jnp.concatenate(parts, axis=1) for parts in (dqs, dks, dvs))
    sums_out[...] = jnp.concatenate(
        [jnp.sum(dq, axis=0, keepdims=True), jnp.sum(dv, axis=0, keepdims=True)], axis=0
    )
    dqkv = jnp.concatenate([jnp.zeros_like(dq), dq, dk, dv], axis=1).astype(BF16)
    dqkv_out[...] = dqkv
    loading[1].wait()
    da = dot_t(dqkv, proj[...])
    if not carried:
        store_blocks(partials, da, dhs[0].shape[0])
        return
    rows = dhs[0].shape[0]
    partials[0][...] = da[:rows]
    for k, (out, ref) in enumerate(zip(partials[1:], carried), 1):
        out[:rows] = da[k * rows : (k + 1) * rows].astype(BF16)
        out[rows:] = ref[...]


def attn_grads_body(layer, dp, meta, x, dh, a, oqkv, dqkv_ref, weights, sums_mid, hidden_sum, qv_sums, *refs):
    outs, (full, proj, sems) = refs[:-3], refs[-3:]
    loading = attn_load(layer, weights, proj, sems)
    width = proj.shape[1] // 4
    dqkv = dqkv_ref[...]
    grad = t_dot(a[...], dqkv)
    grad_o = t_dot(dh[...], oqkv[:, :width])
    full[...] = jnp.concatenate([grad_o, grad[:, width:]], axis=1)
    wait_all(loading)
    da = dot_t(dqkv, proj[...])
    normed, _ = norm_rows(x[...].astype(F32))
    sums = jnp.concatenate(
        [
            jnp.sum(da * normed, axis=0, keepdims=True),
            jnp.sum(da, axis=0, keepdims=True),
            sums_mid[...],
            hidden_sum[...],
        ],
        axis=0,
    )
    rows = full.shape[0] // dp
    half = rows // 2
    first = meta[0] == 0
    beyond = jnp.zeros((7, full.shape[1]), F32)
    fill = lambda v: jnp.concatenate([v, jnp.zeros((v.shape[0], full.shape[1] - v.shape[1]), F32)], axis=1)
    for j in range(dp):
        little = jnp.concatenate(
            [fill(sums[:, j * rows : (j + 1) * rows]), fill(qv_sums[...]), beyond], axis=0
        )
        low, high = (full[(2 * j + i) * half : (2 * j + i + 1) * half] for i in range(2))
        if len(outs) == 1:
            outs[0][j] = jnp.concatenate([low, high, little], axis=0).astype(BF16)
        else:
            for out, values in zip(outs, (jnp.where(first, low, high), jnp.where(first, high, low))):
                out[j] = jnp.concatenate([values, little], axis=0).astype(BF16)


def last_body(n, *refs):
    dh, x, own, others, params = refs[0], refs[1], refs[2], refs[3 : n + 2], refs[n + 2]
    h, y_own, y_params, out, y_out = refs[n + 3 :]
    rows = own.shape[0]
    da, y = own[...], h[...] + y_own[...] + y_params[5:6]
    for ref in others:
        da = da + ref[:rows].astype(F32)
        y = y + ref[rows:].astype(F32)
    y_out[...] = y.astype(BF16)
    normed, inverse = norm_rows(x[...].astype(F32))
    out[...] = dh[...] + norm_back(da, normed, inverse, params[0:1])


def end_back_body(n, *refs):
    dh, x, own, others, params = refs[0], refs[1], refs[2], refs[3 : n + 2], refs[n + 2]
    out, low_out = refs[n + 3 :]
    da = summed(own, others)
    normed, inverse = norm_rows(x[...].astype(F32))
    grad = dh[...] + norm_back(da, normed, inverse, params[0:1])
    out[...] = grad
    low_out[...] = grad.astype(BF16)


def prepare_body(meta, w_qkv, w_out, w_fc1, w_fc2, attn_out, keep, send):
    attn_out[...] = jnp.concatenate([w_out[...].T, w_qkv[0], w_qkv[1], w_qkv[2]], axis=1)
    half = keep.shape[1]
    first = meta[0] == 0
    for g, values in enumerate((w_fc1[...], w_fc2[...])):
        low, high = values[:half], values[half:]
        keep[g] = jnp.where(first, low, high)
        send[g] = jnp.where(first, high, low)


def params_body(meta, mine, other, *outs):
    first = meta[0] == 0
    for out, flipped in zip(outs, (False, True)):
        pair = (other, mine) if flipped else (mine, other)
        values = [jnp.where(first, pair[0][j].astype(F32), pair[1][j].astype(F32)) for j in range(mine.shape[0])]
        out[0:7] = jnp.concatenate([v[0:7] for v in values], axis=1)
        cols = out.shape[1] // 4 // len(values)
        none = jnp.zeros((1, cols * len(values)), F32)
        out[7:8] = jnp.concatenate(
            [none, *(v[7:8, :cols] for v in values), none, *(v[8:9, :cols] for v in values)], axis=1
        )


def join_body(dp, *refs):
    keeps, sends, out = refs[: len(refs) // 2], refs[len(refs) // 2 : -1], refs[-1]
    for j in range(dp):
        out[j] = jnp.concatenate(
            [
                (keep[j].astype(F32) + send[j].astype(F32)).astype(BF16)
                for keep, send in zip(keeps, sends)
            ],
            axis=0,
        )


def split_body(meta, grad, received, own, *outs):
    for k, out in enumerate((own, *outs)):
        j = meta[1] ^ k
        out[...] = (grad[j].astype(F32) + received[j].astype(F32)).astype(out.dtype)


def turn_body(meta, mlp_1, mix, out):
    rows, half = mlp_1.shape[0], mlp_1.shape[0] // 2
    first = meta[0] == 0
    out[:rows] = jnp.where(first, mlp_1[...], mix[:rows])
    out[rows:] = mix[rows : rows + half]


def small_body(count, meta, mix, own, *refs):
    others, little, pieces = refs[:count], refs[count], refs[count + 1 :]
    total = mix[mix.shape[0] - 16 :].astype(F32)
    alone = own[own.shape[0] - 16 :]
    for ref in others:
        alone = alone + ref[ref.shape[0] - 16 :].astype(F32)
    total = jnp.where(meta[0] == 0, alone, total)
    little[...] = total
    share = pieces[0].shape[1]
    for k, out in enumerate(pieces):
        blocks = [
            jnp.where(meta[2] ^ k == j, total[0:6, j * share : (j + 1) * share], 0.0)
            for j in range(len(pieces))
        ]
        out[...] = sum(blocks[1:], blocks[0])


def finish_body(count, meta, mlp_1, mix, received, own, *refs):
    others, (qkv_out, out_out, fc1_out, fc2_out, attn) = refs[:count], refs[count:]
    first = meta[0] == 0
    rows, half = mlp_1.shape[0], mlp_1.shape[0] // 2

    def both(mine, theirs):
        mine, theirs = mine.astype(F32), theirs.astype(F32)
        return jnp.concatenate(
            [jnp.where(first, mine, theirs), jnp.where(first, theirs, mine)], axis=0
        )

    for out, at in ((fc1_out, slice(0, half)), (fc2_out, slice(half, rows))):
        out[...] = both(jnp.where(first, mix[at], mlp_1[at]), received[at])
    last = slice(rows, rows + half)

    @pl.when(first)
    def _():
        total = own[:rows]
        for ref in others:
            total = total + ref[:rows].astype(F32)
        attn[...] = total

    @pl.when(jnp.logical_not(first))
    def _():
        attn[...] = both(mix[last], received[last])

    width = attn.shape[1] // 4
    values = attn[...]
    out_out[...] = values[:, :width].T
    for i in range(3):
        qkv_out[i] = values[:, (i + 1) * width : (i + 2) * width]


def shards(sizes, inputs, cotangent, segments, row_params, qv_bias, w_qkv, w_out, fc1_bias, w_fc1, w_fc2):
    sections, dp, tensor = sizes
    s, d, t = (lax.axis_index(axis) for axis in ("section", "dp", "tensor"))
    smem = pl.BlockSpec(memory_space=pltpu.SMEM)
    vmem = pl.BlockSpec(memory_space=pltpu.VMEM)
    hbm = pl.BlockSpec(memory_space=pltpu.HBM)
    rows, width = inputs.shape[2], inputs.shape[3]
    tokens = rows * tensor
    head_cols, hidden = w_qkv.shape[3], w_fc1.shape[2]
    direct = dp <= 4 and w_qkv.shape[3] * dp == inputs.shape[3]
    pieces = dp if direct else 1
    meta = jnp.stack([s, d, t]).astype(jnp.int32)
    layer_first = s == 0

    def to_tensor(values):
        return [
            lax.ppermute(v, "tensor", [(i, i ^ k) for i in range(tensor)])
            for k, v in enumerate(values, 1)
        ]

    def everywhere(own):
        return [own, *to_tensor([own] * (tensor - 1))]

    def to_dp(values, layer):
        return [
            lax.ppermute(
                v, ("section", "dp"), [(layer * dp + i, layer * dp + (i ^ k)) for i in range(dp)]
            )
            for k, v in enumerate(values, 1)
        ]

    def to_other(value, source):
        return lax.ppermute(value, "section", [(source, 1 - source)])

    def pull(v, i):
        return lax.dynamic_index_in_dim(v, i, 0, keepdims=False, allow_negative_indices=False)

    mine = lambda v: pull(v[0], s)
    xs = everywhere(mine(inputs))
    cots = everywhere(mine(cotangent))
    ids = mine(segments).reshape(tensor, rows)
    order = [t ^ k for k in range(tensor)]
    ids = jnp.concatenate([pull(ids, i) for i in order])
    place = jnp.concatenate([i * rows + jnp.arange(rows, dtype=jnp.int32) for i in order])
    mask = ((ids[:, None] == ids[None, :]) & (place[None, :] <= place[:, None])).astype(F32)

    piece = width // dp
    pad = lambda v: jnp.pad(v, ((0, 0), (0, piece - v.shape[1])))
    small = jnp.concatenate([row_params[0], fc1_bias[0], pad(qv_bias[0, :, 0])], axis=0)
    small = jnp.pad(small, ((0, 16 - small.shape[0]), (0, 0)))
    if direct:
        found = [
            small,
            *(lax.ppermute(small, "dp", [(i, i ^ k) for i in range(dp)]) for k in range(1, dp)),
        ]
        small = jnp.stack(
            [sum(jnp.where(d ^ k == j, v, jnp.zeros_like(v)) for k, v in enumerate(found)) for j in range(dp)]
        )
    else:
        small = lax.all_gather(small, "dp", axis=0)
    other = lax.ppermute(small, "section", [(0, 1), (1, 0)])
    if direct:
        smalls = call(
            params_body, [struct((8, width), F32)] * 2, "params", 0, [meta, small, other],
            [smem, vmem, vmem],
        )
    else:
        smalls = []
        for values in (jnp.where(layer_first, small, other), jnp.where(layer_first, other, small)):
            values = values.astype(F32)
            whole = values.transpose(1, 0, 2).reshape(16, width)
            qv = values[:, 7:9, : head_cols // dp].transpose(1, 0, 2).reshape(2, head_cols)
            none = jnp.zeros((1, head_cols), F32)
            bias = jnp.concatenate([none, qv[0:1], none, qv[1:2]], axis=1)
            smalls.append(jnp.concatenate([whole[:7], bias], axis=0))

    half = piece // 2
    attn_piece, keep, send = call(
        prepare_body,
        [struct((piece, 4 * head_cols), BF16)] + [struct((2, half, hidden), BF16)] * 2,
        "prepare", 0, [meta, *(far(v) for v in (w_qkv[0], w_out[0], w_fc1[0], w_fc2[0].T))],
        [smem] + [vmem] * 4,
    )
    here = ("section", "dp")
    attn_w = far(lax.all_gather(attn_piece, here, axis=0, tiled=True).reshape(2, width, -1))
    other = lax.ppermute(send, "section", [(0, 1), (1, 0)])
    mlp_w = []
    for part in (jnp.where(layer_first, keep, other), jnp.where(layer_first, other, keep)):
        whole = lax.all_gather(part.reshape(2 * half, hidden), here, axis=0, tiled=True)
        whole = whole.reshape(2, dp, 2, half, hidden)
        if half % 16:
            whole = whole.transpose(2, 1, 0, 3, 4).reshape(1, 1, 2, width, hidden)
        mlp_w.append(far(whole))
    stacks, count, _, part_rows, _ = mlp_w[0].shape
    mlp_room = [
        pltpu.VMEM((2, count, stacks * part_rows, hidden), BF16),
        pltpu.SemaphoreType.DMA((stacks, 2)),
    ]

    attn_room = [pltpu.VMEM((width, 4 * head_cols), BF16), pltpu.SemaphoreType.DMA((2,))]
    blocks = [struct((rows, width), F32)] + [struct((rows, width), BF16)] * (tensor - 1)
    late_blocks = [kept(v.shape, v.dtype) for v in blocks]
    unit = 2 * tokens * width * width

    saved = []
    outputs = []
    for layer in range(2):
        params = smalls[layer]
        x_all, a, oqkv, lse, own, *away = call(
            functools.partial(attn_fwd_body, tensor, layer),
            [
                kept((tokens, width), BF16),
                kept((tokens, width), BF16),
                kept((tokens, 4 * head_cols), BF16),
                kept((tokens, head_cols // HEAD_DIM), F32),
                *blocks,
            ],
            "attn_fwd", 2 * unit, [*xs, params, mask, attn_w],
            [vmem] * (tensor + 2) + [hbm], attn_room,
        )
        h, c = call(
            functools.partial(middle_body, tensor),
            [kept((rows, width), F32), struct((rows, width), BF16)],
            "middle", 0, [xs[0], own, *to_tensor(away), params],
        )
        late = layer == 1
        c_all, m, der, own, *away = call(
            functools.partial(mlp_fwd_body, tensor),
            [
                kept((tokens, width), BF16),
                kept((tokens, hidden), BF16),
                kept((tokens, hidden), F32),
                *(late_blocks if late else blocks),
            ],
            "mlp_fwd", 2 * unit, [*everywhere(c), params, mlp_w[layer]],
            [vmem] * (tensor + 1) + [hbm], mlp_room,
        )
        saved.append((xs[0], x_all, a, oqkv, lse, h, c_all, m, der))
        if late:
            carried = (own, away)
            continue
        (y,) = call(
            functools.partial(end_body, tensor),
            [struct((rows, width), BF16)],
            "end", 0, [far(h), own, *to_tensor(away), params],
        )
        outputs.append(y)
        xs = everywhere(y)

    swap = lambda v: lax.ppermute(v, "section", [(0, 1), (1, 0)])

    def joined_halves(pairs, after=()):
        keeps, sends = [p[0] for p in pairs], [swap(p[1]) for p in pairs]
        rows_each = sum(k.shape[1] for k in keeps)
        (joined,) = call(
            functools.partial(join_body, dp),
            [struct((dp, rows_each, hidden), BF16)],
            "join", 0, [*keeps, *sends], after=after,
        )
        return joined

    def over_dp(joined):
        joined = joined.reshape(-1, hidden)
        return lax.psum_scatter(joined, "dp", scatter_dimension=0, tiled=True)

    input_grads = [None] * 2
    pairs = []
    extra = []
    e, es = cots[0], cots
    for layer in (1, 0):
        params = smalls[layer]
        x, x_all, a, oqkv, lse, h, c_all, m, der = saved[layer]
        e_all, du, hidden_sum, own, *away = call(
            functools.partial(mlp_bwd_body, tensor),
            [
                kept((tokens, width), BF16),
                kept((tokens, hidden), BF16),
                kept((1, hidden), F32),
                *blocks,
            ],
            "mlp_bwd", 2 * unit, [*es, far(der), mlp_w[layer]],
            [vmem] * (tensor + 1) + [hbm], mlp_room, extra,
        )
        received = to_tensor(away)
        mlp_grads = functools.partial(
            call,
            functools.partial(mlp_grads_body, dp),
            [struct((dp, 2 * half, hidden), BF16)] * 2,
            "mlp_grads", 2 * unit, [meta, far(c_all), far(e_all), far(du), far(m)],
            [smem] + [vmem] * 4, [pltpu.VMEM((2, width, hidden), F32)],
        )
        mlp_pair = mlp_grads(received)
        dh, dh_low, sums_mid = call(
            functools.partial(middle_back_body, tensor),
            [kept((rows, width), F32), struct((rows, width), BF16), kept((4, width), F32)],
            "middle_back", 0, [e, far(h), own, *received, params],
            after=[mlp_pair[0]],
        )
        dhs = everywhere(dh_low)
        if layer == 1:
            joined = joined_halves([mlp_pair], dhs[1:])
            mlp_1 = over_dp(joined)
        else:
            joined = joined_halves([mlp_pair, *pairs], [*dhs[1:], mlp_1])
            mix = over_dp(joined)
        dh_all, dqkv, qv_sums, own, *away = call(
            functools.partial(attn_bwd_body, tensor, layer),
            [
                kept((tokens, width), BF16),
                kept((tokens, 4 * head_cols), BF16),
                kept((2, head_cols), F32),
                blocks[0],
                *[struct((rows if layer == 1 else 2 * rows, width), BF16)] * (tensor - 1),
            ],
            "attn_bwd", 2 * unit,
            [*dhs, attn_w, far(oqkv), far(lse), mask, *(() if layer == 1 else map(far, carried[1]))],
            [vmem] * tensor + [hbm] + [vmem] * (3 if layer == 1 else tensor + 2),
            attn_room, [joined],
        )
        received = to_tensor(away)
        whole = direct and layer == 0
        attn_grads = functools.partial(
            call,
            functools.partial(attn_grads_body, layer, dp),
            [struct((dp, piece + 16, 4 * head_cols), BF16)]
            if whole
            else [struct((dp, half + 16, 4 * head_cols), BF16)] * 2,
            "attn_grads", 3 * unit,
            [
                meta, far(x_all), far(dh_all), far(a), far(oqkv), far(dqkv), attn_w,
                far(sums_mid), far(hidden_sum), far(qv_sums),
            ],
            [smem] + [vmem] * 5 + [hbm] + [vmem] * 3,
            [pltpu.VMEM((width, 4 * head_cols), F32), *attn_room],
        )
        if layer == 1:
            pass
        elif direct:
            (grad,) = attn_grads()
            attn_own, *attn_away = call(
                split_body,
                [struct((piece + 16, hidden), F32)]
                + [struct((piece + 16, hidden), BF16)] * (dp - 1),
                "split", 0, [meta, grad, to_other(grad, 1)], [smem, vmem, vmem],
            )
            attn_others = to_dp(attn_away, 0)
            follows = attn_own
        else:
            attn_0 = over_dp(joined_halves([attn_grads()]))
            there = swap(attn_0)
            attn_own = jnp.concatenate(
                [jnp.where(layer_first, v[:half], w[:half]) for v, w in ((attn_0, there), (there, attn_0))]
                + [attn_0[half:]]
            ).astype(F32)
            attn_others = []
            follows = attn_own
        if layer == 1:
            e, e_low = call(
                functools.partial(end_back_body, tensor),
                [struct((rows, width), F32), struct((rows, width), BF16)],
                "end_back", 0, [far(dh), x, own, *received, params],
            )
            es = everywhere(e_low)
            attn_pair = attn_grads(es[1:2])
            pairs.append(attn_pair)
            extra = [attn_pair[0]]
        else:
            e, y = call(
                functools.partial(last_body, tensor),
                [struct((rows, width), F32), struct((rows, width), BF16)],
                "last", 0,
                [far(dh), x, own, *received, params, far(saved[1][5]), far(carried[0]), smalls[1]],
                after=[follows],
            )
            outputs.append(y)
        input_grads[layer] = e

    pick = lambda pair: jnp.where(layer_first, pair[0], pair[1])
    flip = lambda pair: jnp.where(layer_first, pair[1], pair[0])
    def both(pair):
        here, there = pick(pair), swap(flip(pair))
        return jnp.stack([jnp.where(layer_first, here, there), jnp.where(layer_first, there, here)])[None, None]

    block_out = both(outputs)
    grads_out = both(input_grads)
    share = piece // tensor
    (sent,) = call(
        turn_body, [struct((3 * half, hidden), BF16)], "turn", 0, [meta, mlp_1, mix],
        [smem, vmem, vmem],
    )
    received = swap(sent)
    total, row_own, *row_away = call(
        functools.partial(small_body, len(attn_others)),
        [struct((16, width), F32)] + [struct((6, share), F32)] * tensor,
        "small", 0, [meta, mix, attn_own, *attn_others],
        [smem] + [vmem] * (2 + len(attn_others)),
    )
    row_grad = row_own + sum(to_tensor(row_away))
    qv_cols = head_cols // dp
    qv_grad = lax.dynamic_slice(
        total, (7, d * qv_cols), (2, qv_cols), allow_negative_indices=False
    )
    w_qkv_grad, w_out_grad, w_fc1_grad, w_fc2_grad = call(
        functools.partial(finish_body, len(attn_others)),
        [
            struct((3, piece, head_cols), F32),
            struct((head_cols, piece), F32),
            struct((piece, hidden), F32),
            struct((piece, hidden), F32),
        ],
        "finish", 0, [meta, mlp_1, mix, received, attn_own, *attn_others],
        [smem] + [vmem] * (4 + len(attn_others)),
        [pltpu.VMEM((piece, 4 * head_cols), F32)],
    )
    return (
        block_out,
        grads_out,
        row_grad[None],
        qv_grad.reshape(1, 2, 1, qv_cols),
        w_qkv_grad[None],
        w_out_grad[None],
        total[6:7, :piece][None],
        w_fc1_grad[None],
        w_fc2_grad.T[None],
    )


def solution(mesh):
    sizes = tuple(mesh.shape[axis] for axis in ("section", "dp", "tensor"))
    placed = (
        P("dp", None, "tensor", None),
        P("dp", None, "tensor", None),
        P("dp", None, None),
        P("section", None, "dp"),
        P("section", None, "tensor", "dp"),
        P("section", None, "dp", "tensor"),
        P("section", "tensor", "dp"),
        P("section", "tensor", "dp"),
        P("section", "dp", "tensor"),
        P("section", "tensor", "dp"),
    )
    return jax.shard_map(
        functools.partial(shards, sizes),
        mesh=mesh,
        in_specs=placed,
        out_specs=(
            P("section", "dp", None, "tensor", None),
            P("section", "dp", None, "tensor", None),
            P("section", None, ("dp", "tensor")),
            P("section", None, "tensor", "dp"),
            P("section", None, "dp", "tensor"),
            P("section", "tensor", "dp"),
            P("section", "tensor", "dp"),
            P("section", "dp", "tensor"),
            P("section", "tensor", "dp"),
        ),
        check_vma=False,
    )
```

```python
import dataclasses
import functools
import math

import jax
import jax.numpy as jnp
from jax import lax
from jax.experimental import pallas as pl
from jax.experimental.pallas import tpu as pltpu
from jax.sharding import PartitionSpec as P

HEAD_DIM = 64
EPSILON = 1e-05
NEG_LARGE = -1e30
GELU_SCALE = 0.7978845608028654
GELU_CUBIC = 0.044715
F32 = jnp.float32
BF16 = jnp.bfloat16
VMEM_LIMIT = 20 * 1024 * 1024


def dot(left, right):
    return jnp.dot(left, right, preferred_element_type=F32)


def dot_t(left, right):
    return lax.dot_general(left, right, (((1,), (1,)), ((), ())), preferred_element_type=F32)


def t_dot(left, right):
    return lax.dot_general(left, right, (((0,), (0,)), ((), ())), preferred_element_type=F32)


def norm_rows(values):
    center = values - jnp.mean(values, axis=-1, keepdims=True)
    inverse = lax.rsqrt(jnp.mean(center * center, axis=-1, keepdims=True) + EPSILON)
    return center * inverse, inverse


def norm_back(grads, normed, inverse, gain):
    scaled = grads * gain
    return inverse * (
        scaled
        - jnp.mean(scaled, axis=-1, keepdims=True)
        - normed * jnp.mean(scaled * normed, axis=-1, keepdims=True)
    )


def rows_of(refs):
    return jnp.concatenate([ref[...] for ref in refs], axis=0)


def store_blocks(outs, values, rows):
    for k, out in enumerate(outs):
        out[...] = values[k * rows : (k + 1) * rows].astype(out.dtype)


def summed(own, others):
    total = own[...]
    for ref in others:
        total = total + ref[...].astype(F32)
    return total


def struct(shape, dtype):
    return jax.ShapeDtypeStruct(shape, dtype)


@dataclasses.dataclass
class Far:
    array: jax.Array


@dataclasses.dataclass
class Kept:
    shape: tuple
    dtype: type


class Fetched:
    def __init__(self, source, room, sem):
        self.room, self.waiting, self.shape = room, True, room.shape
        self.copy = pltpu.make_async_copy(source, room, sem)
        self.copy.start()

    def ready(self):
        if self.waiting:
            self.copy.wait()
        self.waiting = False

    def __getitem__(self, at):
        self.ready()
        return self.room[at]


class Streamed:
    def __init__(self, room, out, sem):
        self.room, self.shape, self.dtype = room, room.shape, room.dtype
        self.copy = pltpu.make_async_copy(room, out, sem)

    def __setitem__(self, at, value):
        self.room[at] = value
        self.copy.start()


def distant(array):
    return pltpu.with_memory_space_constraint(array, pltpu.HBM)


def call(body, outs, name, flops, args, specs=None, scratch=(), after=()):
    vmem, hbm = (pl.BlockSpec(memory_space=m) for m in (pltpu.VMEM, pltpu.HBM))
    specs = list(specs or [vmem] * len(args))
    heavy = name in ("mlp_bwd", "attn_bwd")
    far = [i for i, a in enumerate(args) if heavy and isinstance(a, Far)]
    late = [i for i, o in enumerate(outs) if heavy and isinstance(o, Kept)]
    args = [distant(a.array) if isinstance(a, Far) else a for a in args]
    for i in far:
        specs[i] = hbm
    rooms = [pltpu.VMEM(v.shape, v.dtype) for v in (*(args[i] for i in far), *(outs[i] for i in late))]
    count = len(args)

    def kernel(*refs):
        ins, refs = list(refs[:count]), refs[count + len(after) :]
        results, refs = list(refs[: len(outs)]), refs[len(outs) :]
        own, spaces, sems = refs[: len(scratch)], refs[len(scratch) : -1], refs[-1]
        for k, i in enumerate(far):
            ins[i] = Fetched(ins[i], spaces[k], sems.at[k])
        for k, i in enumerate(late, len(far)):
            results[i] = Streamed(spaces[k], results[i], sems.at[k])
        body(*ins, *results, *own)
        for i in far:
            ins[i].ready()
        for i in late:
            results[i].copy.wait()

    return pl.pallas_call(
        kernel,
        out_shape=tuple(pltpu.HBM(o.shape, o.dtype) if isinstance(o, Kept) else o for o in outs),
        in_specs=specs + [pl.BlockSpec(memory_space=pl.ANY)] * len(after),
        out_specs=tuple(hbm if i in late else vmem for i in range(len(outs))),
        scratch_shapes=[*scratch, *rooms, pltpu.SemaphoreType.DMA((max(1, len(rooms)),))],
        compiler_params=pltpu.CompilerParams(vmem_limit_bytes=VMEM_LIMIT),
        cost_estimate=pl.CostEstimate(
            flops=flops,
            bytes_accessed=sum(math.prod(v.shape) * v.dtype.itemsize for v in args),
            transcendentals=0,
        ),
        name=name,
    )(*args, *after)


def attn_load(layer, weights, proj, sems):
    split = proj.shape[1] // 3
    copies = [
        pltpu.make_async_copy(weights.at[layer, :, at], proj.at[:, at], sems.at[i])
        for i, at in enumerate((pl.ds(0, split), pl.ds(split, 2 * split)))
    ]
    for copy in copies:
        copy.start()
    return copies


def mlp_load(weights, proj, sems, order):
    halves, rows = weights.shape[0], weights.shape[3]
    copies = [
        pltpu.make_async_copy(
            weights.at[i, :, g], proj.at[g, :, pl.ds(i * rows, rows), :], sems.at[i, g]
        )
        for g in order
        for i in range(halves)
    ]
    for copy in copies:
        copy.start()
    return copies[:halves], copies[halves:]


def wait_all(copies):
    for copy in copies:
        copy.wait()


def mlp_weight(proj, g):
    return proj[g].reshape(-1, proj.shape[-1])


def attn_fwd_body(n, layer, *refs):
    xs, (params, mask, weights), refs = refs[:n], refs[n : n + 3], refs[n + 3 :]
    (x_out, a_out, oqkv_out, lse_out), partials, (proj, sem) = refs[:4], refs[4:-2], refs[-2:]
    loading = attn_load(layer, weights, proj, sem)
    x = rows_of(xs)
    x_out[...] = x
    normed, _ = norm_rows(x.astype(F32))
    a = (normed * params[0:1] + params[1:2]).astype(BF16)
    a_out[...] = a
    width = proj.shape[1] // 4
    wait_all(loading)
    oqkv = (dot(a, proj[...]) + params[7:8]).astype(BF16)
    allowed = mask[...] > 0.5
    heads, logs = [], []
    for h in range(width // HEAD_DIM):
        q, k, v = (
            oqkv[:, (1 + i) * width + h * HEAD_DIM : (1 + i) * width + (h + 1) * HEAD_DIM]
            for i in range(3)
        )
        scores = jnp.where(allowed, dot_t(q, k) * HEAD_DIM**-0.5, NEG_LARGE)
        top = jnp.max(scores, axis=-1, keepdims=True)
        powers = jnp.exp(scores - top)
        total = jnp.sum(powers, axis=-1, keepdims=True)
        logs.append(top + jnp.log(total))
        heads.append(dot((powers * (1.0 / total)).astype(BF16), v).astype(BF16))
    o = jnp.concatenate(heads, axis=1)
    oqkv_out[...] = jnp.concatenate([o, oqkv[:, width:]], axis=1)
    blank = jnp.zeros((mask.shape[0], 128 - len(logs)), F32)
    lse_out[...] = jnp.concatenate([*logs, blank], axis=1)
    store_blocks(partials, dot_t(o, proj[:, :width]), xs[0].shape[0])


def middle_body(n, *refs):
    x, own, others, params, h_out, c_out = refs[0], refs[1], refs[2 : n + 1], *refs[n + 1 :]
    h = x[...].astype(F32) + summed(own, others) + params[2:3]
    h_out[...] = h
    normed, _ = norm_rows(h)
    c_out[...] = (normed * params[3:4] + params[4:5]).astype(BF16)


def mlp_fwd_body(n, *refs):
    cs, (params, weights) = refs[:n], refs[n : n + 2]
    c_out, m_out, der_out = refs[n + 2 : n + 5]
    partials, (proj, sems) = refs[n + 5 : -2], refs[-2:]
    first, second = mlp_load(weights, proj, sems, (0, 1))
    c = rows_of(cs)
    c_out[...] = c
    wait_all(first)
    u = dot(c, mlp_weight(proj, 0)) + params[6:7]
    tangent = jnp.tanh(GELU_SCALE * (u + GELU_CUBIC * u * u * u))
    m = (0.5 * u * (1.0 + tangent)).astype(BF16)
    der_out[...] = 0.5 * (1.0 + tangent) + 0.5 * u * (1.0 - tangent * tangent) * GELU_SCALE * (
        1.0 + 3.0 * GELU_CUBIC * u * u
    )
    m_out[...] = m
    wait_all(second)
    store_blocks(partials, dot_t(m, mlp_weight(proj, 1)), cs[0].shape[0])


def end_body(n, *refs):
    h, own, others, params, out = refs[0], refs[1], refs[2 : n + 1], *refs[n + 1 :]
    out[...] = (h[...] + summed(own, others) + params[5:6]).astype(BF16)


def mlp_bwd_body(n, *refs):
    es, (der, weights) = refs[:n], refs[n : n + 2]
    e_out, du_out, sum_out = refs[n + 2 : n + 5]
    partials, (proj, sems) = refs[n + 5 : -2], refs[-2:]
    first, second = mlp_load(weights, proj, sems, (1, 0))
    e = rows_of(es)
    e_out[...] = e
    wait_all(first)
    du = dot(e, mlp_weight(proj, 1)) * der[...]
    du_low = du.astype(BF16)
    du_out[...] = du_low
    sum_out[...] = jnp.sum(du, axis=0, keepdims=True)
    wait_all(second)
    store_blocks(partials, dot_t(du_low, mlp_weight(proj, 0)), es[0].shape[0])


def mlp_grads_body(dp, meta, c, e, du, m, keep, send, full):
    full[0] = t_dot(c[...], du[...])
    full[1] = t_dot(e[...], m[...])
    half = full.shape[1] // dp // 2
    first = meta[0] == 0
    for j in range(dp):
        for g in range(2):
            low, high = (full[g, (2 * j + i) * half : (2 * j + i + 1) * half].astype(BF16) for i in range(2))
            at = slice(g * half, (g + 1) * half)
            keep[j, at] = jnp.where(first, low, high)
            send[j, at] = jnp.where(first, high, low)


def middle_back_body(n, *refs):
    e, h, own, others, params = refs[0], refs[1], refs[2], refs[3 : n + 2], refs[n + 2]
    dh_out, low_out, sums_out = refs[n + 3 :]
    dc = summed(own, others)
    e_values = e[...].astype(F32)
    normed, inverse = norm_rows(h[...])
    dh = e_values + norm_back(dc, normed, inverse, params[3:4])
    dh_out[...] = dh
    low_out[...] = dh.astype(BF16)
    sums_out[...] = jnp.concatenate(
        [jnp.sum(v, axis=0, keepdims=True) for v in (dh, dc * normed, dc, e_values)], axis=0
    )


def attn_bwd_body(n, layer, *refs):
    carried = refs[n + 4 : 2 * n + 3] if layer == 0 else ()
    refs = refs[: n + 4] + refs[n + 4 + len(carried) :]
    dhs, (weights, oqkv_ref, lse, mask) = refs[:n], refs[n : n + 4]
    dh_out, dqkv_out, sums_out = refs[n + 4 : n + 7]
    partials, (proj, sem) = refs[n + 7 : -2], refs[-2:]
    loading = attn_load(layer, weights, proj, sem)
    dh = rows_of(dhs)
    dh_out[...] = dh
    loading[0].wait()
    width = proj.shape[1] // 4
    scale = HEAD_DIM**-0.5
    do = dot(dh, proj[:, :width]).astype(BF16)
    oqkv = oqkv_ref[...]
    allowed = mask[...] > 0.5
    lse = lse[...]
    dqs, dks, dvs = [], [], []
    for h in range(width // HEAD_DIM):
        q, k, v = (
            oqkv[:, (1 + i) * width + h * HEAD_DIM : (1 + i) * width + (h + 1) * HEAD_DIM]
            for i in range(3)
        )
        do_h = do[:, h * HEAD_DIM : (h + 1) * HEAD_DIM]
        scores = jnp.where(allowed, dot_t(q, k) * scale, NEG_LARGE)
        probs = jnp.exp(scores - lse[:, h : h + 1])
        dvs.append(t_dot(probs.astype(BF16), do_h))
        dp = dot_t(do_h, v)
        delta = jnp.sum(probs * dp, axis=-1, keepdims=True)
        ds = (probs * (dp - delta) * scale).astype(BF16)
        dqs.append(dot(ds, k))
        dks.append(t_dot(ds, q))
    dq, dk, dv = (jnp.concatenate(parts, axis=1) for parts in (dqs, dks, dvs))
    sums_out[...] = jnp.concatenate(
        [jnp.sum(dq, axis=0, keepdims=True), jnp.sum(dv, axis=0, keepdims=True)], axis=0
    )
    dqkv = jnp.concatenate([jnp.zeros_like(dq), dq, dk, dv], axis=1).astype(BF16)
    dqkv_out[...] = dqkv
    loading[1].wait()
    da = dot_t(dqkv, proj[...])
    if not carried:
        store_blocks(partials, da, dhs[0].shape[0])
        return
    rows = dhs[0].shape[0]
    partials[0][...] = da[:rows]
    for k, (out, ref) in enumerate(zip(partials[1:], carried), 1):
        out[...] = jnp.concatenate([da[k * rows : (k + 1) * rows].astype(BF16), ref[...]], axis=0)


def attn_grads_body(layer, dp, meta, x, dh, a, oqkv, dqkv_ref, weights, sums_mid, hidden_sum, qv_sums, *refs):
    outs, (full, proj, sems) = refs[:-3], refs[-3:]
    loading = attn_load(layer, weights, proj, sems)
    width = proj.shape[1] // 4
    dqkv = dqkv_ref[...]
    grad = t_dot(a[...], dqkv)
    grad_o = t_dot(dh[...], oqkv[:, :width])
    full[...] = jnp.concatenate([grad_o, grad[:, width:]], axis=1)
    wait_all(loading)
    da = dot_t(dqkv, proj[...])
    normed, _ = norm_rows(x[...].astype(F32))
    sums = jnp.concatenate(
        [
            jnp.sum(da * normed, axis=0, keepdims=True),
            jnp.sum(da, axis=0, keepdims=True),
            sums_mid[...],
            hidden_sum[...],
        ],
        axis=0,
    )
    rows = full.shape[0] // dp
    half = rows // 2
    first = meta[0] == 0
    beyond = jnp.zeros((7, full.shape[1]), F32)
    fill = lambda v: jnp.concatenate([v, jnp.zeros((v.shape[0], full.shape[1] - v.shape[1]), F32)], axis=1)
    for j in range(dp):
        little = jnp.concatenate(
            [fill(sums[:, j * rows : (j + 1) * rows]), fill(qv_sums[...]), beyond], axis=0
        )
        low, high = (full[(2 * j + i) * half : (2 * j + i + 1) * half] for i in range(2))
        if len(outs) == 1:
            outs[0][j] = jnp.concatenate([low, high, little], axis=0).astype(BF16)
        else:
            for out, values in zip(outs, (jnp.where(first, low, high), jnp.where(first, high, low))):
                out[j] = jnp.concatenate([values, little], axis=0).astype(BF16)


def last_body(n, *refs):
    dh, x, own, others, params = refs[0], refs[1], refs[2], refs[3 : n + 2], refs[n + 2]
    h, y_own, y_params, out, y_out = refs[n + 3 :]
    rows = own.shape[0]
    da, y = own[...], h[...] + y_own[...] + y_params[5:6]
    for ref in others:
        da = da + ref[:rows].astype(F32)
        y = y + ref[rows:].astype(F32)
    y_out[...] = y.astype(BF16)
    normed, inverse = norm_rows(x[...].astype(F32))
    out[...] = dh[...] + norm_back(da, normed, inverse, params[0:1])


def end_back_body(n, *refs):
    dh, x, own, others, params = refs[0], refs[1], refs[2], refs[3 : n + 2], refs[n + 2]
    out, low_out = refs[n + 3 :]
    da = summed(own, others)
    normed, inverse = norm_rows(x[...].astype(F32))
    grad = dh[...] + norm_back(da, normed, inverse, params[0:1])
    out[...] = grad
    low_out[...] = grad.astype(BF16)


def prepare_body(meta, w_qkv, w_out, w_fc1, w_fc2, attn_out, keep, send):
    attn_out[...] = jnp.concatenate([w_out[...].T, w_qkv[0], w_qkv[1], w_qkv[2]], axis=1)
    half = keep.shape[1]
    first = meta[0] == 0
    for g, values in enumerate((w_fc1[...], w_fc2[...])):
        low, high = values[:half], values[half:]
        keep[g] = jnp.where(first, low, high)
        send[g] = jnp.where(first, high, low)


def params_body(meta, mine, other, *outs):
    first = meta[0] == 0
    for out, flipped in zip(outs, (False, True)):
        pair = (other, mine) if flipped else (mine, other)
        values = [jnp.where(first, pair[0][j].astype(F32), pair[1][j].astype(F32)) for j in range(mine.shape[0])]
        out[0:7] = jnp.concatenate([v[0:7] for v in values], axis=1)
        cols = out.shape[1] // 4 // len(values)
        none = jnp.zeros((1, cols * len(values)), F32)
        out[7:8] = jnp.concatenate(
            [none, *(v[7:8, :cols] for v in values), none, *(v[8:9, :cols] for v in values)], axis=1
        )


def join_body(dp, *refs):
    count = (len(refs) - 3) // 2
    keeps, sends = refs[:count], refs[count : 2 * count]
    passing, out, passed = refs[2 * count :]
    passed[...] = passing[...]
    for j in range(dp):
        out[j] = jnp.concatenate(
            [
                (keep[j].astype(F32) + send[j].astype(F32)).astype(BF16)
                for keep, send in zip(keeps, sends)
            ],
            axis=0,
        )


def split_body(meta, grad, received, own, *outs):
    for k, out in enumerate((own, *outs)):
        j = meta[1] ^ k
        out[...] = (grad[j].astype(F32) + received[j].astype(F32)).astype(out.dtype)


def turn_body(meta, mlp_1, mix, out):
    rows, half = mlp_1.shape[0], mlp_1.shape[0] // 2
    first = meta[0] == 0
    out[:rows] = jnp.where(first, mlp_1[...], mix[:rows])
    out[rows:] = mix[rows : rows + half]


def small_body(count, meta, mix, own, *refs):
    others, little, pieces = refs[:count], refs[count], refs[count + 1 :]
    total = mix[mix.shape[0] - 16 :].astype(F32)
    alone = own[own.shape[0] - 16 :]
    for ref in others:
        alone = alone + ref[ref.shape[0] - 16 :].astype(F32)
    total = jnp.where(meta[0] == 0, alone, total)
    little[...] = total
    share = pieces[0].shape[1]
    for k, out in enumerate(pieces):
        blocks = [
            jnp.where(meta[2] ^ k == j, total[0:6, j * share : (j + 1) * share], 0.0)
            for j in range(len(pieces))
        ]
        out[...] = sum(blocks[1:], blocks[0])


def rows_body(own, *refs):
    refs[-1][...] = summed(own, refs[:-1])


def finish_body(count, meta, mlp_1, mix, received, own, *refs):
    others, (qkv_out, out_out, fc1_out, fc2_out, attn) = refs[:count], refs[count:]
    first = meta[0] == 0
    rows, half = mlp_1.shape[0], mlp_1.shape[0] // 2

    def both(mine, theirs):
        mine, theirs = mine.astype(F32), theirs.astype(F32)
        return jnp.concatenate(
            [jnp.where(first, mine, theirs), jnp.where(first, theirs, mine)], axis=0
        )

    for out, at in ((fc1_out, slice(0, half)), (fc2_out, slice(half, rows))):
        out[...] = both(jnp.where(first, mix[at], mlp_1[at]), received[at])
    last = slice(rows, rows + half)

    @pl.when(first)
    def _():
        total = own[:rows]
        for ref in others:
            total = total + ref[:rows].astype(F32)
        attn[...] = total

    @pl.when(jnp.logical_not(first))
    def _():
        attn[...] = both(mix[last], received[last])

    width = attn.shape[1] // 4
    values = attn[...]
    out_out[...] = values[:, :width].T
    for i in range(3):
        qkv_out[i] = values[:, (i + 1) * width : (i + 2) * width]


def shards(sizes, inputs, cotangent, segments, row_params, qv_bias, w_qkv, w_out, fc1_bias, w_fc1, w_fc2):
    sections, dp, tensor = sizes
    s, d, t = (lax.axis_index(axis) for axis in ("section", "dp", "tensor"))
    smem = pl.BlockSpec(memory_space=pltpu.SMEM)
    vmem = pl.BlockSpec(memory_space=pltpu.VMEM)
    hbm = pl.BlockSpec(memory_space=pltpu.HBM)
    rows, width = inputs.shape[2], inputs.shape[3]
    tokens = rows * tensor
    head_cols, hidden = w_qkv.shape[3], w_fc1.shape[2]
    direct = dp <= 4 and w_qkv.shape[3] * dp == inputs.shape[3]
    pieces = dp if direct else 1
    meta = jnp.stack([s, d, t]).astype(jnp.int32)
    layer_first = s == 0

    def to_tensor(values):
        return [
            lax.ppermute(v, "tensor", [(i, i ^ k) for i in range(tensor)])
            for k, v in enumerate(values, 1)
        ]

    def everywhere(own):
        return [own, *to_tensor([own] * (tensor - 1))]

    def to_dp(values, layer):
        return [
            lax.ppermute(
                v, ("section", "dp"), [(layer * dp + i, layer * dp + (i ^ k)) for i in range(dp)]
            )
            for k, v in enumerate(values, 1)
        ]

    def to_other(value, source):
        return lax.ppermute(value, "section", [(source, 1 - source)])

    def pull(v, i):
        return lax.dynamic_index_in_dim(v, i, 0, keepdims=False, allow_negative_indices=False)

    mine = lambda v: pull(v[0], s)
    xs = everywhere(mine(inputs))
    cots = everywhere(mine(cotangent))
    ids = mine(segments).reshape(tensor, rows)
    order = [t ^ k for k in range(tensor)]
    ids = jnp.concatenate([pull(ids, i) for i in order])
    place = jnp.concatenate([i * rows + jnp.arange(rows, dtype=jnp.int32) for i in order])
    mask = ((ids[:, None] == ids[None, :]) & (place[None, :] <= place[:, None])).astype(F32)

    piece = width // dp
    pad = lambda v: jnp.pad(v, ((0, 0), (0, piece - v.shape[1])))
    small = jnp.concatenate([row_params[0], fc1_bias[0], pad(qv_bias[0, :, 0])], axis=0)
    small = jnp.pad(small, ((0, 16 - small.shape[0]), (0, 0)))
    if direct:
        found = [
            small,
            *(lax.ppermute(small, "dp", [(i, i ^ k) for i in range(dp)]) for k in range(1, dp)),
        ]
        small = jnp.stack(
            [sum(jnp.where(d ^ k == j, v, jnp.zeros_like(v)) for k, v in enumerate(found)) for j in range(dp)]
        )
    else:
        small = lax.all_gather(small, "dp", axis=0)
    other = lax.ppermute(small, "section", [(0, 1), (1, 0)])
    if direct:
        smalls = call(
            params_body, [struct((8, width), F32)] * 2, "params", 0, [meta, small, other],
            [smem, vmem, vmem],
        )
    else:
        smalls = []
        for values in (jnp.where(layer_first, small, other), jnp.where(layer_first, other, small)):
            values = values.astype(F32)
            whole = values.transpose(1, 0, 2).reshape(16, width)
            qv = values[:, 7:9, : head_cols // dp].transpose(1, 0, 2).reshape(2, head_cols)
            none = jnp.zeros((1, head_cols), F32)
            bias = jnp.concatenate([none, qv[0:1], none, qv[1:2]], axis=1)
            smalls.append(jnp.concatenate([whole[:7], bias], axis=0))

    half = piece // 2
    attn_piece, keep, send = call(
        prepare_body,
        [struct((piece, 4 * head_cols), BF16)] + [struct((2, half, hidden), BF16)] * 2,
        "prepare", 0, [meta, *(Far(v) for v in (w_qkv[0], w_out[0], w_fc1[0], w_fc2[0].T))],
        [smem] + [vmem] * 4,
    )
    here = ("section", "dp")
    attn_w = distant(lax.all_gather(attn_piece, here, axis=0, tiled=True).reshape(2, width, -1))
    other = lax.ppermute(send, "section", [(0, 1), (1, 0)])
    mlp_w = []
    for part in (jnp.where(layer_first, keep, other), jnp.where(layer_first, other, keep)):
        whole = lax.all_gather(part.reshape(2 * half, hidden), here, axis=0, tiled=True)
        whole = whole.reshape(2, dp, 2, half, hidden)
        if half % 16:
            whole = whole.transpose(2, 1, 0, 3, 4).reshape(1, 1, 2, width, hidden)
        mlp_w.append(distant(whole))
    stacks, count, _, part_rows, _ = mlp_w[0].shape
    mlp_room = [
        pltpu.VMEM((2, count, stacks * part_rows, hidden), BF16),
        pltpu.SemaphoreType.DMA((stacks, 2)),
    ]

    attn_room = [pltpu.VMEM((width, 4 * head_cols), BF16), pltpu.SemaphoreType.DMA((2,))]
    blocks = [struct((rows, width), F32)] + [struct((rows, width), BF16)] * (tensor - 1)
    late_blocks = [Kept(v.shape, v.dtype) for v in blocks]
    unit = 2 * tokens * width * width

    saved = []
    outputs = []
    for layer in range(2):
        params = smalls[layer]
        x_all, a, oqkv, lse, own, *away = call(
            functools.partial(attn_fwd_body, tensor, layer),
            [
                Kept((tokens, width), BF16),
                Kept((tokens, width), BF16),
                Kept((tokens, 4 * head_cols), BF16),
                Kept((tokens, 128), F32),
                *blocks,
            ],
            "attn_fwd", 2 * unit, [*xs, params, mask, attn_w],
            [vmem] * (tensor + 2) + [hbm], attn_room,
        )
        h, c = call(
            functools.partial(middle_body, tensor),
            [Kept((rows, width), F32), struct((rows, width), BF16)],
            "middle", 0, [xs[0], own, *to_tensor(away), params],
        )
        late = layer == 1
        c_all, m, der, own, *away = call(
            functools.partial(mlp_fwd_body, tensor),
            [
                Kept((tokens, width), BF16),
                Kept((tokens, hidden), BF16),
                Kept((tokens, hidden), F32),
                *(late_blocks if late else blocks),
            ],
            "mlp_fwd", 2 * unit, [*everywhere(c), params, mlp_w[layer]],
            [vmem] * (tensor + 1) + [hbm], mlp_room,
        )
        saved.append((xs[0], x_all, a, oqkv, lse, h, c_all, m, der))
        if late:
            carried = (own, away)
            continue
        (y,) = call(
            functools.partial(end_body, tensor),
            [struct((rows, width), BF16)],
            "end", 0, [Far(h), own, *to_tensor(away), params],
        )
        outputs.append(y)
        xs = everywhere(y)

    swap = lambda v: lax.ppermute(v, "section", [(0, 1), (1, 0)])

    def joined_halves(pairs, passing, after=()):
        keeps, sends = [p[0] for p in pairs], [swap(p[1]) for p in pairs]
        rows_each = sum(k.shape[1] for k in keeps)
        return call(
            functools.partial(join_body, dp),
            [struct((dp, rows_each, hidden), BF16), struct(passing.shape, passing.dtype)],
            "join", 0, [keeps[0], *map(distant, keeps[1:]), sends[0], *map(distant, sends[1:]), passing], after=after,
        )

    def over_dp(joined):
        joined = joined.reshape(-1, hidden)
        return lax.psum_scatter(joined, "dp", scatter_dimension=0, tiled=True)

    input_grads = [None] * 2
    pairs = []
    extra = []
    share = piece // tensor
    e, es = cots[0], cots
    for layer in (1, 0):
        params = smalls[layer]
        x, x_all, a, oqkv, lse, h, c_all, m, der = saved[layer]
        e_all, du, hidden_sum, own, *away = call(
            functools.partial(mlp_bwd_body, tensor),
            [
                Kept((tokens, width), BF16),
                Kept((tokens, hidden), BF16),
                struct((1, hidden), F32),
                *blocks,
            ],
            "mlp_bwd", 2 * unit, [*es, Far(der), mlp_w[layer]],
            [vmem] * (tensor + 1) + [hbm], mlp_room, extra,
        )
        received = to_tensor(away)
        mlp_grads = functools.partial(
            call,
            functools.partial(mlp_grads_body, dp),
            [struct((dp, 2 * half, hidden), BF16)] * 2,
            "mlp_grads", 2 * unit, [meta, Far(c_all), Far(e_all), Far(du), Far(m)],
            [smem] + [vmem] * 4, [pltpu.VMEM((2, width, hidden), F32)],
        )
        mlp_pair = mlp_grads(received)
        dh, dh_low, sums_mid = call(
            functools.partial(middle_back_body, tensor),
            [Kept((rows, width), F32), struct((rows, width), BF16), struct((4, width), F32)],
            "middle_back", 0, [e, Far(h), own, *received, params],
            after=[mlp_pair[0]],
        )
        if layer == 1:
            joined, dh_low = joined_halves([mlp_pair], dh_low)
            mlp_1 = over_dp(joined)
        else:
            joined, dh_low = joined_halves([mlp_pair, *pairs], dh_low, [mlp_1])
            mix = over_dp(joined)
        dhs = everywhere(dh_low)
        dh_all, dqkv, qv_sums, own, *away = call(
            functools.partial(attn_bwd_body, tensor, layer),
            [
                Kept((tokens, width), BF16),
                Kept((tokens, 4 * head_cols), BF16),
                struct((2, head_cols), F32),
                blocks[0],
                *[struct((rows if layer == 1 else 2 * rows, width), BF16)] * (tensor - 1),
            ],
            "attn_bwd", 2 * unit,
            [*dhs, attn_w, Far(oqkv), Far(lse), mask, *(() if layer == 1 else map(Far, carried[1]))],
            [vmem] * tensor + [hbm] + [vmem] * (3 if layer == 1 else tensor + 2),
            attn_room,
        )
        received = to_tensor(away)
        whole = direct and layer == 0
        attn_grads = functools.partial(
            call,
            functools.partial(attn_grads_body, layer, dp),
            [struct((dp, piece + 16, 4 * head_cols), BF16)]
            if whole
            else [struct((dp, half + 16, 4 * head_cols), BF16)] * 2,
            "attn_grads", 3 * unit,
            [
                meta, Far(x_all), Far(dh_all), Far(a), Far(oqkv), Far(dqkv), attn_w,
                sums_mid, hidden_sum, qv_sums,
            ],
            [smem] + [vmem] * 5 + [hbm] + [vmem] * 3,
            [pltpu.VMEM((width, 4 * head_cols), F32), *attn_room],
        )
        if layer == 1:
            pass
        elif direct:
            (grad,) = attn_grads()
            attn_own, *attn_away = call(
                split_body,
                [struct((piece + 16, hidden), F32)]
                + [struct((piece + 16, hidden), BF16)] * (dp - 1),
                "split", 0, [meta, grad, to_other(grad, 1)], [smem, vmem, vmem],
            )
            attn_others = to_dp(attn_away, 0)
        else:
            attn_0 = over_dp(joined_halves([attn_grads()], dh_low)[0])
            there = swap(attn_0)
            attn_own = jnp.concatenate(
                [jnp.where(layer_first, v[:half], w[:half]) for v, w in ((attn_0, there), (there, attn_0))]
                + [attn_0[half:]]
            ).astype(F32)
            attn_others = []
        if layer == 1:
            e, e_low = call(
                functools.partial(end_back_body, tensor),
                [struct((rows, width), F32), struct((rows, width), BF16)],
                "end_back", 0, [Far(dh), x, own, *received, params],
            )
            es = everywhere(e_low)
            attn_pair = attn_grads(es[1:2])
            pairs.append(attn_pair)
            extra = [attn_pair[0]]
        else:
            (sent,) = call(
                turn_body, [struct((3 * half, hidden), BF16)], "turn", 0, [meta, mlp_1, mix],
                [smem, vmem, vmem],
            )
            total, row_own, *row_away = call(
                functools.partial(small_body, len(attn_others)),
                [struct((16, width), F32)] + [struct((6, share), F32)] * tensor,
                "small", 0, [meta, mix, attn_own, *attn_others],
                [smem] + [vmem] * (2 + len(attn_others)),
            )
            e, y = call(
                functools.partial(last_body, tensor),
                [struct((rows, width), F32), struct((rows, width), BF16)],
                "last", 0,
                [Far(dh), x, own, *received, params, Far(saved[1][5]), Far(carried[0]), smalls[1]],
                after=[total],
            )
            outputs.append(y)
        input_grads[layer] = e

    pick = lambda pair: jnp.where(layer_first, pair[0], pair[1])
    flip = lambda pair: jnp.where(layer_first, pair[1], pair[0])
    def both(pair):
        here, there = pick(pair), swap(flip(pair))
        return jnp.stack([jnp.where(layer_first, here, there), jnp.where(layer_first, there, here)])[None, None]

    block_out = both(outputs)
    grads_out = both(input_grads)
    received = swap(sent)
    row_away = to_tensor(row_away)
    qv_cols = head_cols // dp
    qv_grad = lax.dynamic_slice(
        total, (7, d * qv_cols), (2, qv_cols), allow_negative_indices=False
    )
    w_qkv_grad, w_out_grad, w_fc1_grad, w_fc2_grad = call(
        functools.partial(finish_body, len(attn_others)),
        [
            struct((3, piece, head_cols), F32),
            struct((head_cols, piece), F32),
            struct((piece, hidden), F32),
            struct((piece, hidden), F32),
        ],
        "finish", 0, [meta, mlp_1, mix, received, attn_own, *attn_others],
        [smem] + [vmem] * (4 + len(attn_others)),
        [pltpu.VMEM((piece, 4 * head_cols), F32)],
    )
    (row_grad,) = call(
        rows_body, [struct((6, share), F32)], "rows", 0, [row_own, *row_away], after=[w_fc1_grad]
    )
    return (
        block_out,
        grads_out,
        row_grad[None],
        qv_grad.reshape(1, 2, 1, qv_cols),
        w_qkv_grad[None],
        w_out_grad[None],
        total[6:7, :piece][None],
        w_fc1_grad[None],
        w_fc2_grad.T[None],
    )


def solution(mesh):
    sizes = tuple(mesh.shape[axis] for axis in ("section", "dp", "tensor"))
    placed = (
        P("dp", None, "tensor", None),
        P("dp", None, "tensor", None),
        P("dp", None, None),
        P("section", None, "dp"),
        P("section", None, "tensor", "dp"),
        P("section", None, "dp", "tensor"),
        P("section", "tensor", "dp"),
        P("section", "tensor", "dp"),
        P("section", "dp", "tensor"),
        P("section", "tensor", "dp"),
    )
    return jax.shard_map(
        functools.partial(shards, sizes),
        mesh=mesh,
        in_specs=placed,
        out_specs=(
            P("section", "dp", None, "tensor", None),
            P("section", "dp", None, "tensor", None),
            P("section", None, ("dp", "tensor")),
            P("section", None, "tensor", "dp"),
            P("section", None, "dp", "tensor"),
            P("section", "tensor", "dp"),
            P("section", "tensor", "dp"),
            P("section", "dp", "tensor"),
            P("section", "tensor", "dp"),
        ),
        check_vma=False,
    )
```

```python
import dataclasses
import functools
import math

import jax
import jax.numpy as jnp
from jax import lax
from jax.experimental import pallas as pl
from jax.experimental.pallas import tpu as pltpu
from jax.sharding import PartitionSpec as P

HEAD_DIM = 64
EPSILON = 1e-05
NEG_LARGE = -1e30
GELU_SCALE = 0.7978845608028654
GELU_CUBIC = 0.044715
F32 = jnp.float32
BF16 = jnp.bfloat16
VMEM_LIMIT = 20 * 1024 * 1024


def dot(left, right):
    return jnp.dot(left, right, preferred_element_type=F32)


def dot_t(left, right):
    return lax.dot_general(left, right, (((1,), (1,)), ((), ())), preferred_element_type=F32)


def t_dot(left, right):
    return lax.dot_general(left, right, (((0,), (0,)), ((), ())), preferred_element_type=F32)


def norm_rows(values):
    center = values - jnp.mean(values, axis=-1, keepdims=True)
    inverse = lax.rsqrt(jnp.mean(center * center, axis=-1, keepdims=True) + EPSILON)
    return center * inverse, inverse


def norm_back(grads, normed, inverse, gain):
    scaled = grads * gain
    return inverse * (
        scaled
        - jnp.mean(scaled, axis=-1, keepdims=True)
        - normed * jnp.mean(scaled * normed, axis=-1, keepdims=True)
    )


def rows_of(refs):
    return jnp.concatenate([ref[...] for ref in refs], axis=0)


def store_blocks(outs, values, rows):
    for k, out in enumerate(outs):
        out[...] = values[k * rows : (k + 1) * rows].astype(out.dtype)


def summed(own, others):
    total = own[...]
    for ref in others:
        total = total + ref[...].astype(F32)
    return total


def struct(shape, dtype):
    return jax.ShapeDtypeStruct(shape, dtype)


@dataclasses.dataclass
class Far:
    array: jax.Array


@dataclasses.dataclass
class Kept:
    shape: tuple
    dtype: type


class Fetched:
    def __init__(self, source, room, sem):
        self.room, self.waiting, self.shape = room, True, room.shape
        self.copy = pltpu.make_async_copy(source, room, sem)
        self.copy.start()

    def ready(self):
        if self.waiting:
            self.copy.wait()
        self.waiting = False

    def __getitem__(self, at):
        self.ready()
        return self.room[at]


class Streamed:
    def __init__(self, room, out, sem):
        self.room, self.shape, self.dtype = room, room.shape, room.dtype
        self.copy = pltpu.make_async_copy(room, out, sem)

    def __setitem__(self, at, value):
        self.room[at] = value
        self.copy.start()


def distant(array):
    return pltpu.with_memory_space_constraint(array, pltpu.HBM)


def call(body, outs, name, flops, args, specs=None, scratch=(), after=()):
    vmem, hbm = (pl.BlockSpec(memory_space=m) for m in (pltpu.VMEM, pltpu.HBM))
    specs = list(specs or [vmem] * len(args))
    heavy = name in ("mlp_bwd", "attn_bwd")
    far = [i for i, a in enumerate(args) if heavy and isinstance(a, Far)]
    late = [i for i, o in enumerate(outs) if heavy and isinstance(o, Kept)]
    args = [distant(a.array) if isinstance(a, Far) else a for a in args]
    for i in far:
        specs[i] = hbm
    rooms = [pltpu.VMEM(v.shape, v.dtype) for v in (*(args[i] for i in far), *(outs[i] for i in late))]
    count = len(args)

    def kernel(*refs):
        ins, refs = list(refs[:count]), refs[count + len(after) :]
        results, refs = list(refs[: len(outs)]), refs[len(outs) :]
        own, spaces, sems = refs[: len(scratch)], refs[len(scratch) : -1], refs[-1]
        for k, i in enumerate(far):
            ins[i] = Fetched(ins[i], spaces[k], sems.at[k])
        for k, i in enumerate(late, len(far)):
            results[i] = Streamed(spaces[k], results[i], sems.at[k])
        body(*ins, *results, *own)
        for i in far:
            ins[i].ready()
        for i in late:
            results[i].copy.wait()

    return pl.pallas_call(
        kernel,
        out_shape=tuple(pltpu.HBM(o.shape, o.dtype) if isinstance(o, Kept) else o for o in outs),
        in_specs=specs + [pl.BlockSpec(memory_space=pl.ANY)] * len(after),
        out_specs=tuple(hbm if i in late else vmem for i in range(len(outs))),
        scratch_shapes=[*scratch, *rooms, pltpu.SemaphoreType.DMA((max(1, len(rooms)),))],
        compiler_params=pltpu.CompilerParams(vmem_limit_bytes=VMEM_LIMIT),
        cost_estimate=pl.CostEstimate(
            flops=flops,
            bytes_accessed=sum(math.prod(v.shape) * v.dtype.itemsize for v in args),
            transcendentals=0,
        ),
        name=name,
    )(*args, *after)


def attn_load(layer, weights, proj, sems):
    split = proj.shape[1] // 3
    copies = [
        pltpu.make_async_copy(weights.at[layer, :, at], proj.at[:, at], sems.at[i])
        for i, at in enumerate((pl.ds(0, split), pl.ds(split, 2 * split)))
    ]
    for copy in copies:
        copy.start()
    return copies


def mlp_load(weights, proj, sems, order):
    halves, rows = weights.shape[0], weights.shape[3]
    copies = [
        pltpu.make_async_copy(
            weights.at[i, :, g], proj.at[g, :, pl.ds(i * rows, rows), :], sems.at[i, g]
        )
        for g in order
        for i in range(halves)
    ]
    for copy in copies:
        copy.start()
    return copies[:halves], copies[halves:]


def wait_all(copies):
    for copy in copies:
        copy.wait()


def mlp_weight(proj, g):
    return proj[g].reshape(-1, proj.shape[-1])


def attn_fwd_body(n, layer, *refs):
    xs, (params, mask, weights), refs = refs[:n], refs[n : n + 3], refs[n + 3 :]
    (x_out, a_out, oqkv_out, lse_out), partials, (proj, sem) = refs[:4], refs[4:-2], refs[-2:]
    loading = attn_load(layer, weights, proj, sem)
    x = rows_of(xs)
    x_out[...] = x
    normed, _ = norm_rows(x.astype(F32))
    a = (normed * params[0:1] + params[1:2]).astype(BF16)
    a_out[...] = a
    width = proj.shape[1] // 4
    wait_all(loading)
    oqkv = (dot(a, proj[...]) + params[7:8]).astype(BF16)
    allowed = mask[...] > 0.5
    heads, logs = [], []
    for h in range(width // HEAD_DIM):
        q, k, v = (
            oqkv[:, (1 + i) * width + h * HEAD_DIM : (1 + i) * width + (h + 1) * HEAD_DIM]
            for i in range(3)
        )
        scores = jnp.where(allowed, dot_t(q, k) * HEAD_DIM**-0.5, NEG_LARGE)
        top = jnp.max(scores, axis=-1, keepdims=True)
        powers = jnp.exp(scores - top)
        total = jnp.sum(powers, axis=-1, keepdims=True)
        logs.append(top + jnp.log(total))
        heads.append(dot((powers * (1.0 / total)).astype(BF16), v).astype(BF16))
    o = jnp.concatenate(heads, axis=1)
    oqkv_out[...] = jnp.concatenate([o, oqkv[:, width:]], axis=1)
    blank = jnp.zeros((mask.shape[0], 128 - len(logs)), F32)
    lse_out[...] = jnp.concatenate([*logs, blank], axis=1)
    store_blocks(partials, dot_t(o, proj[:, :width]), xs[0].shape[0])


def middle_body(n, *refs):
    x, own, others, params, h_out, c_out = refs[0], refs[1], refs[2 : n + 1], *refs[n + 1 :]
    h = x[...].astype(F32) + summed(own, others) + params[2:3]
    h_out[...] = h
    normed, _ = norm_rows(h)
    c_out[...] = (normed * params[3:4] + params[4:5]).astype(BF16)


def mlp_fwd_body(n, *refs):
    cs, (params, weights) = refs[:n], refs[n : n + 2]
    c_out, m_out, der_out = refs[n + 2 : n + 5]
    partials, (proj, sems) = refs[n + 5 : -2], refs[-2:]
    first, second = mlp_load(weights, proj, sems, (0, 1))
    c = rows_of(cs)
    c_out[...] = c
    wait_all(first)
    u = dot(c, mlp_weight(proj, 0)) + params[6:7]
    tangent = jnp.tanh(GELU_SCALE * (u + GELU_CUBIC * u * u * u))
    m = (0.5 * u * (1.0 + tangent)).astype(BF16)
    der_out[...] = 0.5 * (1.0 + tangent) + 0.5 * u * (1.0 - tangent * tangent) * GELU_SCALE * (
        1.0 + 3.0 * GELU_CUBIC * u * u
    )
    m_out[...] = m
    wait_all(second)
    store_blocks(partials, dot_t(m, mlp_weight(proj, 1)), cs[0].shape[0])


def end_body(n, *refs):
    h, own, others, params, out = refs[0], refs[1], refs[2 : n + 1], *refs[n + 1 :]
    out[...] = (h[...] + summed(own, others) + params[5:6]).astype(BF16)


def mlp_bwd_body(n, *refs):
    es, (der, weights) = refs[:n], refs[n : n + 2]
    e_out, du_out, sum_out = refs[n + 2 : n + 5]
    partials, (proj, sems) = refs[n + 5 : -2], refs[-2:]
    first, second = mlp_load(weights, proj, sems, (1, 0))
    e = rows_of(es)
    e_out[...] = e
    wait_all(first)
    du = dot(e, mlp_weight(proj, 1)) * der[...]
    du_low = du.astype(BF16)
    du_out[...] = du_low
    sum_out[...] = jnp.sum(du, axis=0, keepdims=True)
    wait_all(second)
    store_blocks(partials, dot_t(du_low, mlp_weight(proj, 0)), es[0].shape[0])


def mlp_grads_body(dp, meta, c, e, du, m, keep, send, full):
    full[0] = t_dot(c[...], du[...])
    full[1] = t_dot(e[...], m[...])
    half = full.shape[1] // dp // 2
    first = meta[0] == 0
    for j in range(dp):
        for g in range(2):
            low, high = (full[g, (2 * j + i) * half : (2 * j + i + 1) * half].astype(BF16) for i in range(2))
            at = slice(g * half, (g + 1) * half)
            keep[j, at] = jnp.where(first, low, high)
            send[j, at] = jnp.where(first, high, low)


def middle_back_body(n, *refs):
    e, h, own, others, params = refs[0], refs[1], refs[2], refs[3 : n + 2], refs[n + 2]
    dh_out, low_out, sums_out = refs[n + 3 :]
    dc = summed(own, others)
    e_values = e[...].astype(F32)
    normed, inverse = norm_rows(h[...])
    dh = e_values + norm_back(dc, normed, inverse, params[3:4])
    dh_out[...] = dh
    low_out[...] = dh.astype(BF16)
    sums_out[...] = jnp.concatenate(
        [jnp.sum(v, axis=0, keepdims=True) for v in (dh, dc * normed, dc, e_values)], axis=0
    )


def attn_bwd_body(n, layer, *refs):
    carried = refs[n + 4 : 2 * n + 3] if layer == 0 else ()
    refs = refs[: n + 4] + refs[n + 4 + len(carried) :]
    dhs, (weights, oqkv_ref, lse, mask) = refs[:n], refs[n : n + 4]
    dh_out, dqkv_out, sums_out = refs[n + 4 : n + 7]
    partials, (proj, sem) = refs[n + 7 : -2], refs[-2:]
    loading = attn_load(layer, weights, proj, sem)
    dh = rows_of(dhs)
    dh_out[...] = dh
    loading[0].wait()
    width = proj.shape[1] // 4
    scale = HEAD_DIM**-0.5
    do = dot(dh, proj[:, :width]).astype(BF16)
    oqkv = oqkv_ref[...]
    allowed = mask[...] > 0.5
    lse = lse[...]
    dqs, dks, dvs = [], [], []
    for h in range(width // HEAD_DIM):
        q, k, v = (
            oqkv[:, (1 + i) * width + h * HEAD_DIM : (1 + i) * width + (h + 1) * HEAD_DIM]
            for i in range(3)
        )
        do_h = do[:, h * HEAD_DIM : (h + 1) * HEAD_DIM]
        scores = jnp.where(allowed, dot_t(q, k) * scale, NEG_LARGE)
        probs = jnp.exp(scores - lse[:, h : h + 1])
        dvs.append(t_dot(probs.astype(BF16), do_h))
        dp = dot_t(do_h, v)
        delta = jnp.sum(probs * dp, axis=-1, keepdims=True)
        ds = (probs * (dp - delta) * scale).astype(BF16)
        dqs.append(dot(ds, k))
        dks.append(t_dot(ds, q))
    dq, dk, dv = (jnp.concatenate(parts, axis=1) for parts in (dqs, dks, dvs))
    sums_out[...] = jnp.concatenate(
        [jnp.sum(dq, axis=0, keepdims=True), jnp.sum(dv, axis=0, keepdims=True)], axis=0
    )
    dqkv = jnp.concatenate([jnp.zeros_like(dq), dq, dk, dv], axis=1).astype(BF16)
    dqkv_out[...] = dqkv
    loading[1].wait()
    da = dot_t(dqkv, proj[...])
    if not carried:
        store_blocks(partials, da, dhs[0].shape[0])
        return
    rows = dhs[0].shape[0]
    partials[0][...] = da[:rows]
    for k, (out, ref) in enumerate(zip(partials[1:], carried), 1):
        out[...] = jnp.concatenate([da[k * rows : (k + 1) * rows].astype(BF16), ref[...]], axis=0)


def attn_grads_body(layer, dp, meta, x, dh, a, oqkv, dqkv_ref, weights, sums_mid, hidden_sum, qv_sums, *refs):
    outs, (full, proj, sems) = refs[:-3], refs[-3:]
    loading = attn_load(layer, weights, proj, sems)
    width = proj.shape[1] // 4
    dqkv = dqkv_ref[...]
    grad = t_dot(a[...], dqkv)
    grad_o = t_dot(dh[...], oqkv[:, :width])
    full[...] = jnp.concatenate([grad_o, grad[:, width:]], axis=1)
    wait_all(loading)
    da = dot_t(dqkv, proj[...])
    normed, _ = norm_rows(x[...].astype(F32))
    sums = jnp.concatenate(
        [
            jnp.sum(da * normed, axis=0, keepdims=True),
            jnp.sum(da, axis=0, keepdims=True),
            sums_mid[...],
            hidden_sum[...],
        ],
        axis=0,
    )
    rows = full.shape[0] // dp
    half = rows // 2
    first = meta[0] == 0
    beyond = jnp.zeros((7, full.shape[1]), F32)
    fill = lambda v: jnp.concatenate([v, jnp.zeros((v.shape[0], full.shape[1] - v.shape[1]), F32)], axis=1)
    for j in range(dp):
        little = jnp.concatenate(
            [fill(sums[:, j * rows : (j + 1) * rows]), fill(qv_sums[...]), beyond], axis=0
        )
        low, high = (full[(2 * j + i) * half : (2 * j + i + 1) * half] for i in range(2))
        if len(outs) == 1:
            outs[0][j] = jnp.concatenate([low, high, little], axis=0).astype(BF16)
        else:
            for out, values in zip(outs, (jnp.where(first, low, high), jnp.where(first, high, low))):
                out[j] = jnp.concatenate([values, little], axis=0).astype(BF16)


def last_body(n, *refs):
    dh, x, own, others, params = refs[0], refs[1], refs[2], refs[3 : n + 2], refs[n + 2]
    h, y_own, y_params, out, y_out = refs[n + 3 :]
    rows = own.shape[0]
    da, y = own[...], h[...] + y_own[...] + y_params[5:6]
    for ref in others:
        da = da + ref[:rows].astype(F32)
        y = y + ref[rows:].astype(F32)
    y_out[...] = y.astype(BF16)
    normed, inverse = norm_rows(x[...].astype(F32))
    out[...] = dh[...] + norm_back(da, normed, inverse, params[0:1])


def end_back_body(n, *refs):
    dh, x, own, others, params = refs[0], refs[1], refs[2], refs[3 : n + 2], refs[n + 2]
    out, low_out = refs[n + 3 :]
    da = summed(own, others)
    normed, inverse = norm_rows(x[...].astype(F32))
    grad = dh[...] + norm_back(da, normed, inverse, params[0:1])
    out[...] = grad
    low_out[...] = grad.astype(BF16)


def prepare_body(meta, w_qkv, w_out, w_fc1, w_fc2, attn_out, keep, send):
    attn_out[...] = jnp.concatenate([w_out[...].T, w_qkv[0], w_qkv[1], w_qkv[2]], axis=1)
    half = keep.shape[1]
    first = meta[0] == 0
    for g, values in enumerate((w_fc1[...], w_fc2[...])):
        low, high = values[:half], values[half:]
        keep[g] = jnp.where(first, low, high)
        send[g] = jnp.where(first, high, low)


def params_body(meta, mine, other, *outs):
    first = meta[0] == 0
    for out, flipped in zip(outs, (False, True)):
        pair = (other, mine) if flipped else (mine, other)
        values = [jnp.where(first, pair[0][j].astype(F32), pair[1][j].astype(F32)) for j in range(mine.shape[0])]
        out[0:7] = jnp.concatenate([v[0:7] for v in values], axis=1)
        cols = out.shape[1] // 4 // len(values)
        none = jnp.zeros((1, cols * len(values)), F32)
        out[7:8] = jnp.concatenate(
            [none, *(v[7:8, :cols] for v in values), none, *(v[8:9, :cols] for v in values)], axis=1
        )


def join_body(dp, *refs):
    count = (len(refs) - 3) // 2
    keeps, sends = refs[:count], refs[count : 2 * count]
    passing, out, passed = refs[2 * count :]
    passed[...] = passing[...]
    for j in range(dp):
        out[j] = jnp.concatenate(
            [
                (keep[j].astype(F32) + send[j].astype(F32)).astype(BF16)
                for keep, send in zip(keeps, sends)
            ],
            axis=0,
        )


def split_body(meta, grad, received, own, *outs):
    for k, out in enumerate((own, *outs)):
        j = meta[1] ^ k
        out[...] = (grad[j].astype(F32) + received[j].astype(F32)).astype(out.dtype)


def turn_body(meta, mlp_1, mix, out):
    rows, half = mlp_1.shape[0], mlp_1.shape[0] // 2
    first = meta[0] == 0
    out[:rows] = jnp.where(first, mlp_1[...], mix[:rows])
    out[rows:] = mix[rows : rows + half]


def small_body(count, meta, mix, own, *refs):
    others, little, pieces = refs[:count], refs[count], refs[count + 1 :]
    total = mix[mix.shape[0] - 16 :].astype(F32)
    alone = own[own.shape[0] - 16 :]
    for ref in others:
        alone = alone + ref[ref.shape[0] - 16 :].astype(F32)
    total = jnp.where(meta[0] == 0, alone, total)
    little[...] = total
    share = pieces[0].shape[1]
    for k, out in enumerate(pieces):
        blocks = [
            jnp.where(meta[2] ^ k == j, total[0:6, j * share : (j + 1) * share], 0.0)
            for j in range(len(pieces))
        ]
        out[...] = sum(blocks[1:], blocks[0])


def rows_body(own, *refs):
    refs[-1][...] = summed(own, refs[:-1])


def finish_body(count, meta, mlp_1, mix, received, own, *refs):
    others, (qkv_out, out_out, fc1_out, fc2_out, attn) = refs[:count], refs[count:]
    first = meta[0] == 0
    rows, half = mlp_1.shape[0], mlp_1.shape[0] // 2

    def both(mine, theirs):
        mine, theirs = mine.astype(F32), theirs.astype(F32)
        return jnp.concatenate(
            [jnp.where(first, mine, theirs), jnp.where(first, theirs, mine)], axis=0
        )

    for out, at in ((fc1_out, slice(0, half)), (fc2_out, slice(half, rows))):
        out[...] = both(jnp.where(first, mix[at], mlp_1[at]), received[at])
    last = slice(rows, rows + half)

    @pl.when(first)
    def _():
        total = own[:rows]
        for ref in others:
            total = total + ref[:rows].astype(F32)
        attn[...] = total

    @pl.when(jnp.logical_not(first))
    def _():
        attn[...] = both(mix[last], received[last])

    width = attn.shape[1] // 4
    values = attn[...]
    out_out[...] = values[:, :width].T
    for i in range(3):
        qkv_out[i] = values[:, (i + 1) * width : (i + 2) * width]


def shards(sizes, inputs, cotangent, segments, row_params, qv_bias, w_qkv, w_out, fc1_bias, w_fc1, w_fc2):
    sections, dp, tensor = sizes
    s, d, t = (lax.axis_index(axis) for axis in ("section", "dp", "tensor"))
    smem = pl.BlockSpec(memory_space=pltpu.SMEM)
    vmem = pl.BlockSpec(memory_space=pltpu.VMEM)
    hbm = pl.BlockSpec(memory_space=pltpu.HBM)
    rows, width = inputs.shape[2], inputs.shape[3]
    tokens = rows * tensor
    head_cols, hidden = w_qkv.shape[3], w_fc1.shape[2]
    direct = dp <= 4 and w_qkv.shape[3] * dp == inputs.shape[3]
    pieces = dp if direct else 1
    meta = jnp.stack([s, d, t]).astype(jnp.int32)
    layer_first = s == 0

    def to_tensor(values):
        return [
            lax.ppermute(v, "tensor", [(i, i ^ k) for i in range(tensor)])
            for k, v in enumerate(values, 1)
        ]

    def everywhere(own):
        return [own, *to_tensor([own] * (tensor - 1))]

    def to_dp(values, layer):
        return [
            lax.ppermute(
                v, ("section", "dp"), [(layer * dp + i, layer * dp + (i ^ k)) for i in range(dp)]
            )
            for k, v in enumerate(values, 1)
        ]

    def to_other(value, source):
        return lax.ppermute(value, "section", [(source, 1 - source)])

    def pull(v, i):
        return lax.dynamic_index_in_dim(v, i, 0, keepdims=False, allow_negative_indices=False)

    mine = lambda v: pull(v[0], s)
    xs = everywhere(mine(inputs))
    cots = everywhere(mine(cotangent))
    ids = mine(segments).reshape(tensor, rows)
    order = [t ^ k for k in range(tensor)]
    ids = jnp.concatenate([pull(ids, i) for i in order])
    place = jnp.concatenate([i * rows + jnp.arange(rows, dtype=jnp.int32) for i in order])
    mask = ((ids[:, None] == ids[None, :]) & (place[None, :] <= place[:, None])).astype(F32)

    piece = width // dp
    pad = lambda v: jnp.pad(v, ((0, 0), (0, piece - v.shape[1])))
    small = jnp.concatenate([row_params[0], fc1_bias[0], pad(qv_bias[0, :, 0])], axis=0)
    small = jnp.pad(small, ((0, 16 - small.shape[0]), (0, 0)))
    if direct:
        found = [
            small,
            *(lax.ppermute(small, "dp", [(i, i ^ k) for i in range(dp)]) for k in range(1, dp)),
        ]
        small = jnp.stack(
            [sum(jnp.where(d ^ k == j, v, jnp.zeros_like(v)) for k, v in enumerate(found)) for j in range(dp)]
        )
    else:
        small = lax.all_gather(small, "dp", axis=0)
    other = lax.ppermute(small, "section", [(0, 1), (1, 0)])
    if direct:
        smalls = call(
            params_body, [struct((8, width), F32)] * 2, "params", 0, [meta, small, other],
            [smem, vmem, vmem],
        )
    else:
        smalls = []
        for values in (jnp.where(layer_first, small, other), jnp.where(layer_first, other, small)):
            values = values.astype(F32)
            whole = values.transpose(1, 0, 2).reshape(16, width)
            qv = values[:, 7:9, : head_cols // dp].transpose(1, 0, 2).reshape(2, head_cols)
            none = jnp.zeros((1, head_cols), F32)
            bias = jnp.concatenate([none, qv[0:1], none, qv[1:2]], axis=1)
            smalls.append(jnp.concatenate([whole[:7], bias], axis=0))

    half = piece // 2
    attn_piece, keep, send = call(
        prepare_body,
        [struct((piece, 4 * head_cols), BF16)] + [struct((2, half, hidden), BF16)] * 2,
        "prepare", 0, [meta, *(Far(v) for v in (w_qkv[0], w_out[0], w_fc1[0], w_fc2[0].T))],
        [smem] + [vmem] * 4,
    )
    here = ("section", "dp")
    attn_w = distant(lax.all_gather(attn_piece, here, axis=0, tiled=True).reshape(2, width, -1))
    other = lax.ppermute(send, "section", [(0, 1), (1, 0)])
    mlp_w = []
    for part in (jnp.where(layer_first, keep, other), jnp.where(layer_first, other, keep)):
        whole = lax.all_gather(part.reshape(2 * half, hidden), here, axis=0, tiled=True)
        whole = whole.reshape(2, dp, 2, half, hidden)
        if half % 16:
            whole = whole.transpose(2, 1, 0, 3, 4).reshape(1, 1, 2, width, hidden)
        mlp_w.append(distant(whole))
    stacks, count, _, part_rows, _ = mlp_w[0].shape
    mlp_room = [
        pltpu.VMEM((2, count, stacks * part_rows, hidden), BF16),
        pltpu.SemaphoreType.DMA((stacks, 2)),
    ]

    attn_room = [pltpu.VMEM((width, 4 * head_cols), BF16), pltpu.SemaphoreType.DMA((2,))]
    blocks = [struct((rows, width), F32)] + [struct((rows, width), BF16)] * (tensor - 1)
    late_blocks = [Kept(v.shape, v.dtype) for v in blocks]
    unit = 2 * tokens * width * width

    saved = []
    outputs = []
    for layer in range(2):
        params = smalls[layer]
        x_all, a, oqkv, lse, own, *away = call(
            functools.partial(attn_fwd_body, tensor, layer),
            [
                Kept((tokens, width), BF16),
                Kept((tokens, width), BF16),
                Kept((tokens, 4 * head_cols), BF16),
                Kept((tokens, 128), F32),
                *blocks,
            ],
            "attn_fwd", 2 * unit, [*xs, params, mask, attn_w],
            [vmem] * (tensor + 2) + [hbm], attn_room,
        )
        h, c = call(
            functools.partial(middle_body, tensor),
            [Kept((rows, width), F32), struct((rows, width), BF16)],
            "middle", 0, [xs[0], own, *to_tensor(away), params],
        )
        late = layer == 1
        c_all, m, der, own, *away = call(
            functools.partial(mlp_fwd_body, tensor),
            [
                Kept((tokens, width), BF16),
                Kept((tokens, hidden), BF16),
                Kept((tokens, hidden), F32),
                *(late_blocks if late else blocks),
            ],
            "mlp_fwd", 2 * unit, [*everywhere(c), params, mlp_w[layer]],
            [vmem] * (tensor + 1) + [hbm], mlp_room,
        )
        saved.append((xs[0], x_all, a, oqkv, lse, h, c_all, m, der))
        if late:
            carried = (own, away)
            continue
        (y,) = call(
            functools.partial(end_body, tensor),
            [struct((rows, width), BF16)],
            "end", 0, [Far(h), own, *to_tensor(away), params],
        )
        outputs.append(y)
        xs = everywhere(y)

    swap = lambda v: lax.ppermute(v, "section", [(0, 1), (1, 0)])

    def joined_halves(pairs, passing, after=()):
        keeps, sends = [p[0] for p in pairs], [swap(p[1]) for p in pairs]
        rows_each = sum(k.shape[1] for k in keeps)
        return call(
            functools.partial(join_body, dp),
            [struct((dp, rows_each, hidden), BF16), struct(passing.shape, passing.dtype)],
            "join", 0, [keeps[0], *map(distant, keeps[1:]), *sends, passing], after=after,
        )

    def over_dp(joined):
        joined = joined.reshape(-1, hidden)
        return lax.psum_scatter(joined, "dp", scatter_dimension=0, tiled=True)

    input_grads = [None] * 2
    pairs = []
    extra = []
    share = piece // tensor
    e, es = cots[0], cots
    for layer in (1, 0):
        params = smalls[layer]
        x, x_all, a, oqkv, lse, h, c_all, m, der = saved[layer]
        e_all, du, hidden_sum, own, *away = call(
            functools.partial(mlp_bwd_body, tensor),
            [
                Kept((tokens, width), BF16),
                Kept((tokens, hidden), BF16),
                struct((1, hidden), F32),
                *blocks,
            ],
            "mlp_bwd", 2 * unit, [*es, Far(der), mlp_w[layer]],
            [vmem] * (tensor + 1) + [hbm], mlp_room, extra,
        )
        received = to_tensor(away)
        mlp_grads = functools.partial(
            call,
            functools.partial(mlp_grads_body, dp),
            [struct((dp, 2 * half, hidden), BF16)] * 2,
            "mlp_grads", 2 * unit, [meta, Far(c_all), Far(e_all), Far(du), Far(m)],
            [smem] + [vmem] * 4, [pltpu.VMEM((2, width, hidden), F32)],
        )
        mlp_pair = mlp_grads(received)
        dh, dh_low, sums_mid = call(
            functools.partial(middle_back_body, tensor),
            [Kept((rows, width), F32), struct((rows, width), BF16), Kept((4, width), F32)],
            "middle_back", 0, [e, Far(h), own, *received, params],
            after=[mlp_pair[0]],
        )
        if layer == 1:
            joined, dh_low = joined_halves([mlp_pair], dh_low)
            mlp_1 = over_dp(joined)
        else:
            joined, dh_low = joined_halves([mlp_pair, *pairs], dh_low, [distant(mlp_1)])
            mix = over_dp(joined)
        dhs = everywhere(dh_low)
        dh_all, dqkv, qv_sums, own, *away = call(
            functools.partial(attn_bwd_body, tensor, layer),
            [
                Kept((tokens, width), BF16),
                Kept((tokens, 4 * head_cols), BF16),
                struct((2, head_cols), F32),
                blocks[0],
                *[struct((rows if layer == 1 else 2 * rows, width), BF16)] * (tensor - 1),
            ],
            "attn_bwd", 2 * unit,
            [*dhs, attn_w, Far(oqkv), Far(lse), mask, *(() if layer == 1 else map(Far, carried[1]))],
            [vmem] * tensor + [hbm] + [vmem] * (3 if layer == 1 else tensor + 2),
            attn_room,
        )
        received = to_tensor(away)
        whole = direct and layer == 0
        attn_grads = functools.partial(
            call,
            functools.partial(attn_grads_body, layer, dp),
            [struct((dp, piece + 16, 4 * head_cols), BF16)]
            if whole
            else [struct((dp, half + 16, 4 * head_cols), BF16)] * 2,
            "attn_grads", 3 * unit,
            [
                meta, Far(x_all), Far(dh_all), Far(a), Far(oqkv), Far(dqkv), attn_w,
                distant(sums_mid), hidden_sum, qv_sums,
            ],
            [smem] + [vmem] * 5 + [hbm] + [vmem] * 3,
            [pltpu.VMEM((width, 4 * head_cols), F32), *attn_room],
        )
        if layer == 1:
            pass
        elif direct:
            (grad,) = attn_grads()
            attn_own, *attn_away = call(
                split_body,
                [struct((piece + 16, hidden), F32)]
                + [struct((piece + 16, hidden), BF16)] * (dp - 1),
                "split", 0, [meta, grad, to_other(grad, 1)], [smem, vmem, vmem],
            )
            attn_others = to_dp(attn_away, 0)
        else:
            attn_0 = over_dp(joined_halves([attn_grads()], dh_low)[0])
            there = swap(attn_0)
            attn_own = jnp.concatenate(
                [jnp.where(layer_first, v[:half], w[:half]) for v, w in ((attn_0, there), (there, attn_0))]
                + [attn_0[half:]]
            ).astype(F32)
            attn_others = []
        if layer == 1:
            e, e_low = call(
                functools.partial(end_back_body, tensor),
                [struct((rows, width), F32), struct((rows, width), BF16)],
                "end_back", 0, [Far(dh), x, own, *received, params],
            )
            es = everywhere(e_low)
            attn_pair = attn_grads(es[1:2])
            pairs.append(attn_pair)
            extra = [attn_pair[0]]
        else:
            (sent,) = call(
                turn_body, [struct((3 * half, hidden), BF16)], "turn", 0, [meta, mlp_1, mix],
                [smem, vmem, vmem],
            )
            total, row_own, *row_away = call(
                functools.partial(small_body, len(attn_others)),
                [struct((16, width), F32)] + [struct((6, share), F32)] * tensor,
                "small", 0, [meta, mix, attn_own, *attn_others],
                [smem] + [vmem] * (2 + len(attn_others)),
            )
            e, y = call(
                functools.partial(last_body, tensor),
                [struct((rows, width), F32), struct((rows, width), BF16)],
                "last", 0,
                [Far(dh), x, own, *received, params, Far(saved[1][5]), Far(carried[0]), smalls[1]],
                after=[total],
            )
            outputs.append(y)
        input_grads[layer] = e

    pick = lambda pair: jnp.where(layer_first, pair[0], pair[1])
    flip = lambda pair: jnp.where(layer_first, pair[1], pair[0])
    def both(pair):
        here, there = pick(pair), swap(flip(pair))
        return jnp.stack([jnp.where(layer_first, here, there), jnp.where(layer_first, there, here)])[None, None]

    block_out = both(outputs)
    grads_out = both(input_grads)
    received = swap(sent)
    row_away = to_tensor(row_away)
    qv_cols = head_cols // dp
    qv_grad = lax.dynamic_slice(
        total, (7, d * qv_cols), (2, qv_cols), allow_negative_indices=False
    )
    w_qkv_grad, w_out_grad, w_fc1_grad, w_fc2_grad = call(
        functools.partial(finish_body, len(attn_others)),
        [
            struct((3, piece, head_cols), F32),
            struct((head_cols, piece), F32),
            struct((piece, hidden), F32),
            struct((piece, hidden), F32),
        ],
        "finish", 0, [meta, mlp_1, mix, received, attn_own, *attn_others],
        [smem] + [vmem] * (4 + len(attn_others)),
        [pltpu.VMEM((piece, 4 * head_cols), F32)],
    )
    (row_grad,) = call(
        rows_body, [struct((6, share), F32)], "rows", 0, [row_own, *row_away], after=[w_fc1_grad]
    )
    return (
        block_out,
        grads_out,
        row_grad[None],
        qv_grad.reshape(1, 2, 1, qv_cols),
        w_qkv_grad[None],
        w_out_grad[None],
        total[6:7, :piece][None],
        w_fc1_grad[None],
        w_fc2_grad.T[None],
    )


def solution(mesh):
    sizes = tuple(mesh.shape[axis] for axis in ("section", "dp", "tensor"))
    placed = (
        P("dp", None, "tensor", None),
        P("dp", None, "tensor", None),
        P("dp", None, None),
        P("section", None, "dp"),
        P("section", None, "tensor", "dp"),
        P("section", None, "dp", "tensor"),
        P("section", "tensor", "dp"),
        P("section", "tensor", "dp"),
        P("section", "dp", "tensor"),
        P("section", "tensor", "dp"),
    )
    return jax.shard_map(
        functools.partial(shards, sizes),
        mesh=mesh,
        in_specs=placed,
        out_specs=(
            P("section", "dp", None, "tensor", None),
            P("section", "dp", None, "tensor", None),
            P("section", None, ("dp", "tensor")),
            P("section", None, "tensor", "dp"),
            P("section", None, "dp", "tensor"),
            P("section", "tensor", "dp"),
            P("section", "tensor", "dp"),
            P("section", "dp", "tensor"),
            P("section", "tensor", "dp"),
        ),
        check_vma=False,
    )
```

```python
import dataclasses
import functools
import math

import jax
import jax.numpy as jnp
from jax import lax
from jax.experimental import pallas as pl
from jax.experimental.pallas import tpu as pltpu
from jax.sharding import PartitionSpec as P

HEAD_DIM = 64
EPSILON = 1e-05
NEG_LARGE = -1e30
GELU_SCALE = 0.7978845608028654
GELU_CUBIC = 0.044715
F32 = jnp.float32
BF16 = jnp.bfloat16
VMEM_LIMIT = 20 * 1024 * 1024


def dot(left, right):
    return jnp.dot(left, right, preferred_element_type=F32)


def dot_t(left, right):
    return lax.dot_general(left, right, (((1,), (1,)), ((), ())), preferred_element_type=F32)


def t_dot(left, right):
    return lax.dot_general(left, right, (((0,), (0,)), ((), ())), preferred_element_type=F32)


def norm_rows(values):
    center = values - jnp.mean(values, axis=-1, keepdims=True)
    inverse = lax.rsqrt(jnp.mean(center * center, axis=-1, keepdims=True) + EPSILON)
    return center * inverse, inverse


def norm_back(grads, normed, inverse, gain):
    scaled = grads * gain
    return inverse * (
        scaled
        - jnp.mean(scaled, axis=-1, keepdims=True)
        - normed * jnp.mean(scaled * normed, axis=-1, keepdims=True)
    )


def rows_of(refs):
    return jnp.concatenate([ref[...] for ref in refs], axis=0)


def store_blocks(outs, values, rows):
    for k, out in enumerate(outs):
        out[...] = values[k * rows : (k + 1) * rows].astype(out.dtype)


def summed(own, others):
    total = own[...]
    for ref in others:
        total = total + ref[...].astype(F32)
    return total


def struct(shape, dtype):
    return jax.ShapeDtypeStruct(shape, dtype)


@dataclasses.dataclass
class Far:
    array: jax.Array


@dataclasses.dataclass
class Kept:
    shape: tuple
    dtype: type


class Fetched:
    def __init__(self, source, room, sem):
        self.room, self.waiting, self.shape = room, True, room.shape
        self.copy = pltpu.make_async_copy(source, room, sem)
        self.copy.start()

    def ready(self):
        if self.waiting:
            self.copy.wait()
        self.waiting = False

    def __getitem__(self, at):
        self.ready()
        return self.room[at]


class Streamed:
    def __init__(self, room, out, sem):
        self.room, self.shape, self.dtype = room, room.shape, room.dtype
        self.copy = pltpu.make_async_copy(room, out, sem)

    def __setitem__(self, at, value):
        self.room[at] = value
        self.copy.start()


def distant(array):
    return pltpu.with_memory_space_constraint(array, pltpu.HBM)


def call(body, outs, name, flops, args, specs=None, scratch=(), after=()):
    vmem, hbm = (pl.BlockSpec(memory_space=m) for m in (pltpu.VMEM, pltpu.HBM))
    specs = list(specs or [vmem] * len(args))
    heavy = name in ("mlp_bwd", "attn_bwd")
    far = [i for i, a in enumerate(args) if heavy and isinstance(a, Far)]
    late = [i for i, o in enumerate(outs) if heavy and isinstance(o, Kept)]
    args = [distant(a.array) if isinstance(a, Far) else a for a in args]
    for i in far:
        specs[i] = hbm
    rooms = [pltpu.VMEM(v.shape, v.dtype) for v in (*(args[i] for i in far), *(outs[i] for i in late))]
    count = len(args)

    def kernel(*refs):
        ins, refs = list(refs[:count]), refs[count + len(after) :]
        results, refs = list(refs[: len(outs)]), refs[len(outs) :]
        own, spaces, sems = refs[: len(scratch)], refs[len(scratch) : -1], refs[-1]
        for k, i in enumerate(far):
            ins[i] = Fetched(ins[i], spaces[k], sems.at[k])
        for k, i in enumerate(late, len(far)):
            results[i] = Streamed(spaces[k], results[i], sems.at[k])
        body(*ins, *results, *own)
        for i in far:
            ins[i].ready()
        for i in late:
            results[i].copy.wait()

    return pl.pallas_call(
        kernel,
        out_shape=tuple(pltpu.HBM(o.shape, o.dtype) if isinstance(o, Kept) else o for o in outs),
        in_specs=specs + [pl.BlockSpec(memory_space=pl.ANY)] * len(after),
        out_specs=tuple(hbm if i in late else vmem for i in range(len(outs))),
        scratch_shapes=[*scratch, *rooms, pltpu.SemaphoreType.DMA((max(1, len(rooms)),))],
        compiler_params=pltpu.CompilerParams(vmem_limit_bytes=VMEM_LIMIT),
        cost_estimate=pl.CostEstimate(
            flops=flops,
            bytes_accessed=sum(math.prod(v.shape) * v.dtype.itemsize for v in args),
            transcendentals=0,
        ),
        name=name,
    )(*args, *after)


def attn_load(layer, weights, proj, sems):
    split = proj.shape[1] // 3
    copies = [
        pltpu.make_async_copy(weights.at[layer, :, at], proj.at[:, at], sems.at[i])
        for i, at in enumerate((pl.ds(0, split), pl.ds(split, 2 * split)))
    ]
    for copy in copies:
        copy.start()
    return copies


def mlp_load(weights, proj, sems, order):
    halves, rows = weights.shape[0], weights.shape[3]
    copies = [
        pltpu.make_async_copy(
            weights.at[i, :, g], proj.at[g, :, pl.ds(i * rows, rows), :], sems.at[i, g]
        )
        for g in order
        for i in range(halves)
    ]
    for copy in copies:
        copy.start()
    return copies[:halves], copies[halves:]


def wait_all(copies):
    for copy in copies:
        copy.wait()


def mlp_weight(proj, g):
    return proj[g].reshape(-1, proj.shape[-1])


def attn_fwd_body(n, layer, *refs):
    xs, (params, mask, weights), refs = refs[:n], refs[n : n + 3], refs[n + 3 :]
    (x_out, a_out, oqkv_out, lse_out), partials, (proj, sem) = refs[:4], refs[4:-2], refs[-2:]
    loading = attn_load(layer, weights, proj, sem)
    x = rows_of(xs)
    x_out[...] = x
    normed, _ = norm_rows(x.astype(F32))
    a = (normed * params[0:1] + params[1:2]).astype(BF16)
    a_out[...] = a
    width = proj.shape[1] // 4
    wait_all(loading)
    oqkv = (dot(a, proj[...]) + params[7:8]).astype(BF16)
    allowed = mask[...] > 0.5
    heads, logs = [], []
    for h in range(width // HEAD_DIM):
        q, k, v = (
            oqkv[:, (1 + i) * width + h * HEAD_DIM : (1 + i) * width + (h + 1) * HEAD_DIM]
            for i in range(3)
        )
        scores = jnp.where(allowed, dot_t(q, k) * HEAD_DIM**-0.5, NEG_LARGE)
        top = jnp.max(scores, axis=-1, keepdims=True)
        powers = jnp.exp(scores - top)
        total = jnp.sum(powers, axis=-1, keepdims=True)
        logs.append(top + jnp.log(total))
        heads.append(dot((powers * (1.0 / total)).astype(BF16), v).astype(BF16))
    o = jnp.concatenate(heads, axis=1)
    oqkv_out[...] = jnp.concatenate([o, oqkv[:, width:]], axis=1)
    blank = jnp.zeros((mask.shape[0], 128 - len(logs)), F32)
    lse_out[...] = jnp.concatenate([*logs, blank], axis=1)
    store_blocks(partials, dot_t(o, proj[:, :width]), xs[0].shape[0])


def middle_body(n, *refs):
    x, own, others, params, h_out, c_out = refs[0], refs[1], refs[2 : n + 1], *refs[n + 1 :]
    h = x[...].astype(F32) + summed(own, others) + params[2:3]
    h_out[...] = h
    normed, _ = norm_rows(h)
    c_out[...] = (normed * params[3:4] + params[4:5]).astype(BF16)


def mlp_fwd_body(n, *refs):
    cs, (params, weights) = refs[:n], refs[n : n + 2]
    c_out, m_out, der_out = refs[n + 2 : n + 5]
    partials, (proj, sems) = refs[n + 5 : -2], refs[-2:]
    first, second = mlp_load(weights, proj, sems, (0, 1))
    c = rows_of(cs)
    c_out[...] = c
    wait_all(first)
    u = dot(c, mlp_weight(proj, 0)) + params[6:7]
    tangent = jnp.tanh(GELU_SCALE * (u + GELU_CUBIC * u * u * u))
    m = (0.5 * u * (1.0 + tangent)).astype(BF16)
    der_out[...] = 0.5 * (1.0 + tangent) + 0.5 * u * (1.0 - tangent * tangent) * GELU_SCALE * (
        1.0 + 3.0 * GELU_CUBIC * u * u
    )
    m_out[...] = m
    wait_all(second)
    store_blocks(partials, dot_t(m, mlp_weight(proj, 1)), cs[0].shape[0])


def end_body(n, *refs):
    h, own, others, params, out = refs[0], refs[1], refs[2 : n + 1], *refs[n + 1 :]
    out[...] = (h[...] + summed(own, others) + params[5:6]).astype(BF16)


def mlp_bwd_body(n, *refs):
    es, (der, weights) = refs[:n], refs[n : n + 2]
    e_out, du_out, sum_out = refs[n + 2 : n + 5]
    partials, (proj, sems) = refs[n + 5 : -2], refs[-2:]
    first, second = mlp_load(weights, proj, sems, (1, 0))
    e = rows_of(es)
    e_out[...] = e
    wait_all(first)
    du = dot(e, mlp_weight(proj, 1)) * der[...]
    du_low = du.astype(BF16)
    du_out[...] = du_low
    sum_out[...] = jnp.sum(du, axis=0, keepdims=True)
    wait_all(second)
    store_blocks(partials, dot_t(du_low, mlp_weight(proj, 0)), es[0].shape[0])


def mlp_grads_body(dp, meta, c, e, du, m, keep, send, full):
    full[0] = t_dot(c[...], du[...])
    full[1] = t_dot(e[...], m[...])
    half = full.shape[1] // dp // 2
    first = meta[0] == 0
    for j in range(dp):
        for g in range(2):
            low, high = (full[g, (2 * j + i) * half : (2 * j + i + 1) * half].astype(BF16) for i in range(2))
            at = slice(g * half, (g + 1) * half)
            keep[j, at] = jnp.where(first, low, high)
            send[j, at] = jnp.where(first, high, low)


def middle_back_body(n, *refs):
    e, h, own, others, params = refs[0], refs[1], refs[2], refs[3 : n + 2], refs[n + 2]
    dh_out, low_out, sums_out = refs[n + 3 :]
    dc = summed(own, others)
    e_values = e[...].astype(F32)
    normed, inverse = norm_rows(h[...])
    dh = e_values + norm_back(dc, normed, inverse, params[3:4])
    dh_out[...] = dh
    low_out[...] = dh.astype(BF16)
    sums_out[...] = jnp.concatenate(
        [jnp.sum(v, axis=0, keepdims=True) for v in (dh, dc * normed, dc, e_values)], axis=0
    )


def attn_bwd_body(n, layer, *refs):
    carried = refs[n + 4 : 2 * n + 3] if layer == 0 else ()
    refs = refs[: n + 4] + refs[n + 4 + len(carried) :]
    dhs, (weights, oqkv_ref, lse, mask) = refs[:n], refs[n : n + 4]
    dh_out, dqkv_out, sums_out = refs[n + 4 : n + 7]
    partials, (proj, sem) = refs[n + 7 : -2], refs[-2:]
    loading = attn_load(layer, weights, proj, sem)
    dh = rows_of(dhs)
    dh_out[...] = dh
    loading[0].wait()
    width = proj.shape[1] // 4
    scale = HEAD_DIM**-0.5
    do = dot(dh, proj[:, :width]).astype(BF16)
    oqkv = oqkv_ref[...]
    allowed = mask[...] > 0.5
    lse = lse[...]
    dqs, dks, dvs = [], [], []
    for h in range(width // HEAD_DIM):
        q, k, v = (
            oqkv[:, (1 + i) * width + h * HEAD_DIM : (1 + i) * width + (h + 1) * HEAD_DIM]
            for i in range(3)
        )
        do_h = do[:, h * HEAD_DIM : (h + 1) * HEAD_DIM]
        scores = jnp.where(allowed, dot_t(q, k) * scale, NEG_LARGE)
        probs = jnp.exp(scores - lse[:, h : h + 1])
        dvs.append(t_dot(probs.astype(BF16), do_h))
        dp = dot_t(do_h, v)
        delta = jnp.sum(probs * dp, axis=-1, keepdims=True)
        ds = (probs * (dp - delta) * scale).astype(BF16)
        dqs.append(dot(ds, k))
        dks.append(t_dot(ds, q))
    dq, dk, dv = (jnp.concatenate(parts, axis=1) for parts in (dqs, dks, dvs))
    sums_out[...] = jnp.concatenate(
        [jnp.sum(dq, axis=0, keepdims=True), jnp.sum(dv, axis=0, keepdims=True)], axis=0
    )
    dqkv = jnp.concatenate([jnp.zeros_like(dq), dq, dk, dv], axis=1).astype(BF16)
    dqkv_out[...] = dqkv
    loading[1].wait()
    da = dot_t(dqkv, proj[...])
    if not carried:
        store_blocks(partials, da, dhs[0].shape[0])
        return
    rows = dhs[0].shape[0]
    partials[0][...] = da[:rows]
    for k, (out, ref) in enumerate(zip(partials[1:], carried), 1):
        out[...] = jnp.concatenate([da[k * rows : (k + 1) * rows].astype(BF16), ref[...]], axis=0)


def attn_grads_body(layer, dp, meta, x, dh, a, oqkv, dqkv_ref, weights, sums_mid, hidden_sum, qv_sums, *refs):
    outs, (full, proj, sems) = refs[:-3], refs[-3:]
    loading = attn_load(layer, weights, proj, sems)
    width = proj.shape[1] // 4
    dqkv = dqkv_ref[...]
    grad = t_dot(a[...], dqkv)
    grad_o = t_dot(dh[...], oqkv[:, :width])
    full[...] = jnp.concatenate([grad_o, grad[:, width:]], axis=1)
    wait_all(loading)
    da = dot_t(dqkv, proj[...])
    normed, _ = norm_rows(x[...].astype(F32))
    sums = jnp.concatenate(
        [
            jnp.sum(da * normed, axis=0, keepdims=True),
            jnp.sum(da, axis=0, keepdims=True),
            sums_mid[...],
            hidden_sum[...],
        ],
        axis=0,
    )
    rows = full.shape[0] // dp
    half = rows // 2
    first = meta[0] == 0
    beyond = jnp.zeros((7, full.shape[1]), F32)
    fill = lambda v: jnp.concatenate([v, jnp.zeros((v.shape[0], full.shape[1] - v.shape[1]), F32)], axis=1)
    for j in range(dp):
        little = jnp.concatenate(
            [fill(sums[:, j * rows : (j + 1) * rows]), fill(qv_sums[...]), beyond], axis=0
        )
        low, high = (full[(2 * j + i) * half : (2 * j + i + 1) * half] for i in range(2))
        if len(outs) == 1:
            outs[0][j] = jnp.concatenate([low, high, little], axis=0).astype(BF16)
        else:
            for out, values in zip(outs, (jnp.where(first, low, high), jnp.where(first, high, low))):
                out[j] = jnp.concatenate([values, little], axis=0).astype(BF16)


def last_body(n, *refs):
    dh, x, own, others, params = refs[0], refs[1], refs[2], refs[3 : n + 2], refs[n + 2]
    h, y_own, y_params, out, y_out = refs[n + 3 :]
    rows = own.shape[0]
    da, y = own[...], h[...] + y_own[...] + y_params[5:6]
    for ref in others:
        da = da + ref[:rows].astype(F32)
        y = y + ref[rows:].astype(F32)
    y_out[...] = y.astype(BF16)
    normed, inverse = norm_rows(x[...].astype(F32))
    out[...] = dh[...] + norm_back(da, normed, inverse, params[0:1])


def end_back_body(n, *refs):
    dh, x, own, others, params = refs[0], refs[1], refs[2], refs[3 : n + 2], refs[n + 2]
    out, low_out = refs[n + 3 :]
    da = summed(own, others)
    normed, inverse = norm_rows(x[...].astype(F32))
    grad = dh[...] + norm_back(da, normed, inverse, params[0:1])
    out[...] = grad
    low_out[...] = grad.astype(BF16)


def prepare_attn_body(w_qkv, w_out, attn_out):
    attn_out[...] = jnp.concatenate([w_out[...].T, w_qkv[0], w_qkv[1], w_qkv[2]], axis=1)


def prepare_mlp_body(meta, w_fc1, w_fc2, keep, send):
    half = keep.shape[1]
    first = meta[0] == 0
    for g, values in enumerate((w_fc1[...], w_fc2[...])):
        low, high = values[:half], values[half:]
        keep[g] = jnp.where(first, low, high)
        send[g] = jnp.where(first, high, low)


def params_body(meta, mine, other, *outs):
    first = meta[0] == 0
    for out, flipped in zip(outs, (False, True)):
        pair = (other, mine) if flipped else (mine, other)
        values = [jnp.where(first, pair[0][j].astype(F32), pair[1][j].astype(F32)) for j in range(mine.shape[0])]
        out[0:7] = jnp.concatenate([v[0:7] for v in values], axis=1)
        cols = out.shape[1] // 4 // len(values)
        none = jnp.zeros((1, cols * len(values)), F32)
        out[7:8] = jnp.concatenate(
            [none, *(v[7:8, :cols] for v in values), none, *(v[8:9, :cols] for v in values)], axis=1
        )


def join_body(dp, *refs):
    count = (len(refs) - 3) // 2
    keeps, sends = refs[:count], refs[count : 2 * count]
    passing, out, passed = refs[2 * count :]
    passed[...] = passing[...]
    for j in range(dp):
        out[j] = jnp.concatenate(
            [
                (keep[j].astype(F32) + send[j].astype(F32)).astype(BF16)
                for keep, send in zip(keeps, sends)
            ],
            axis=0,
        )


def split_body(meta, grad, received, own, *outs):
    for k, out in enumerate((own, *outs)):
        j = meta[1] ^ k
        out[...] = (grad[j].astype(F32) + received[j].astype(F32)).astype(out.dtype)


def turn_body(meta, mlp_1, mix, out):
    rows, half = mlp_1.shape[0], mlp_1.shape[0] // 2
    first = meta[0] == 0
    out[:rows] = jnp.where(first, mlp_1[...], mix[:rows])
    out[rows:] = mix[rows : rows + half]


def small_body(count, meta, mix, own, *refs):
    others, little, pieces = refs[:count], refs[count], refs[count + 1 :]
    total = mix[mix.shape[0] - 16 :].astype(F32)
    alone = own[own.shape[0] - 16 :]
    for ref in others:
        alone = alone + ref[ref.shape[0] - 16 :].astype(F32)
    total = jnp.where(meta[0] == 0, alone, total)
    little[...] = total
    share = pieces[0].shape[1]
    for k, out in enumerate(pieces):
        blocks = [
            jnp.where(meta[2] ^ k == j, total[0:6, j * share : (j + 1) * share], 0.0)
            for j in range(len(pieces))
        ]
        out[...] = sum(blocks[1:], blocks[0])


def rows_body(own, *refs):
    refs[-1][...] = summed(own, refs[:-1])


def finish_body(count, meta, mlp_1, mix, received, own, *refs):
    others, (qkv_out, out_out, fc1_out, fc2_out, attn) = refs[:count], refs[count:]
    first = meta[0] == 0
    rows, half = mlp_1.shape[0], mlp_1.shape[0] // 2

    def both(mine, theirs):
        mine, theirs = mine.astype(F32), theirs.astype(F32)
        return jnp.concatenate(
            [jnp.where(first, mine, theirs), jnp.where(first, theirs, mine)], axis=0
        )

    for out, at in ((fc1_out, slice(0, half)), (fc2_out, slice(half, rows))):
        out[...] = both(jnp.where(first, mix[at], mlp_1[at]), received[at])
    last = slice(rows, rows + half)

    @pl.when(first)
    def _():
        total = own[:rows]
        for ref in others:
            total = total + ref[:rows].astype(F32)
        attn[...] = total

    @pl.when(jnp.logical_not(first))
    def _():
        attn[...] = both(mix[last], received[last])

    width = attn.shape[1] // 4
    values = attn[...]
    out_out[...] = values[:, :width].T
    for i in range(3):
        qkv_out[i] = values[:, (i + 1) * width : (i + 2) * width]


def shards(sizes, inputs, cotangent, segments, row_params, qv_bias, w_qkv, w_out, fc1_bias, w_fc1, w_fc2):
    sections, dp, tensor = sizes
    s, d, t = (lax.axis_index(axis) for axis in ("section", "dp", "tensor"))
    smem = pl.BlockSpec(memory_space=pltpu.SMEM)
    vmem = pl.BlockSpec(memory_space=pltpu.VMEM)
    hbm = pl.BlockSpec(memory_space=pltpu.HBM)
    rows, width = inputs.shape[2], inputs.shape[3]
    tokens = rows * tensor
    head_cols, hidden = w_qkv.shape[3], w_fc1.shape[2]
    direct = dp <= 4 and w_qkv.shape[3] * dp == inputs.shape[3]
    pieces = dp if direct else 1
    meta = jnp.stack([s, d, t]).astype(jnp.int32)
    layer_first = s == 0

    def to_tensor(values):
        return [
            lax.ppermute(v, "tensor", [(i, i ^ k) for i in range(tensor)])
            for k, v in enumerate(values, 1)
        ]

    def everywhere(own):
        return [own, *to_tensor([own] * (tensor - 1))]

    def to_dp(values, layer):
        return [
            lax.ppermute(
                v, ("section", "dp"), [(layer * dp + i, layer * dp + (i ^ k)) for i in range(dp)]
            )
            for k, v in enumerate(values, 1)
        ]

    def to_other(value, source):
        return lax.ppermute(value, "section", [(source, 1 - source)])

    def pull(v, i):
        return lax.dynamic_index_in_dim(v, i, 0, keepdims=False, allow_negative_indices=False)

    mine = lambda v: pull(v[0], s)
    xs = everywhere(mine(inputs))
    cots = everywhere(mine(cotangent))
    ids = mine(segments).reshape(tensor, rows)
    order = [t ^ k for k in range(tensor)]
    ids = jnp.concatenate([pull(ids, i) for i in order])
    place = jnp.concatenate([i * rows + jnp.arange(rows, dtype=jnp.int32) for i in order])
    mask = ((ids[:, None] == ids[None, :]) & (place[None, :] <= place[:, None])).astype(F32)

    piece = width // dp
    pad = lambda v: jnp.pad(v, ((0, 0), (0, piece - v.shape[1])))
    small = jnp.concatenate([row_params[0], fc1_bias[0], pad(qv_bias[0, :, 0])], axis=0)
    small = jnp.pad(small, ((0, 16 - small.shape[0]), (0, 0)))
    if direct:
        found = [
            small,
            *(lax.ppermute(small, "dp", [(i, i ^ k) for i in range(dp)]) for k in range(1, dp)),
        ]
        small = jnp.stack(
            [sum(jnp.where(d ^ k == j, v, jnp.zeros_like(v)) for k, v in enumerate(found)) for j in range(dp)]
        )
    else:
        small = lax.all_gather(small, "dp", axis=0)
    other = lax.ppermute(small, "section", [(0, 1), (1, 0)])
    if direct:
        smalls = call(
            params_body, [struct((8, width), F32)] * 2, "params", 0, [meta, small, other],
            [smem, vmem, vmem],
        )
    else:
        smalls = []
        for values in (jnp.where(layer_first, small, other), jnp.where(layer_first, other, small)):
            values = values.astype(F32)
            whole = values.transpose(1, 0, 2).reshape(16, width)
            qv = values[:, 7:9, : head_cols // dp].transpose(1, 0, 2).reshape(2, head_cols)
            none = jnp.zeros((1, head_cols), F32)
            bias = jnp.concatenate([none, qv[0:1], none, qv[1:2]], axis=1)
            smalls.append(jnp.concatenate([whole[:7], bias], axis=0))

    half = piece // 2
    (attn_piece,) = call(
        prepare_attn_body, [struct((piece, 4 * head_cols), BF16)], "prepare_attn", 0,
        [Far(w_qkv[0]), Far(w_out[0])],
    )
    keep, send = call(
        prepare_mlp_body, [struct((2, half, hidden), BF16)] * 2, "prepare_mlp", 0,
        [meta, Far(w_fc1[0]), Far(w_fc2[0].T)], [smem, vmem, vmem], after=[attn_piece],
    )
    here = ("section", "dp")
    attn_w = distant(lax.all_gather(attn_piece, here, axis=0, tiled=True).reshape(2, width, -1))
    other = lax.ppermute(send, "section", [(0, 1), (1, 0)])
    mlp_w = []
    for part in (jnp.where(layer_first, keep, other), jnp.where(layer_first, other, keep)):
        whole = lax.all_gather(part.reshape(2 * half, hidden), here, axis=0, tiled=True)
        whole = whole.reshape(2, dp, 2, half, hidden)
        if half % 16:
            whole = whole.transpose(2, 1, 0, 3, 4).reshape(1, 1, 2, width, hidden)
        mlp_w.append(distant(whole))
    stacks, count, _, part_rows, _ = mlp_w[0].shape
    mlp_room = [
        pltpu.VMEM((2, count, stacks * part_rows, hidden), BF16),
        pltpu.SemaphoreType.DMA((stacks, 2)),
    ]

    attn_room = [pltpu.VMEM((width, 4 * head_cols), BF16), pltpu.SemaphoreType.DMA((2,))]
    blocks = [struct((rows, width), F32)] + [struct((rows, width), BF16)] * (tensor - 1)
    late_blocks = [Kept(v.shape, v.dtype) for v in blocks]
    unit = 2 * tokens * width * width

    saved = []
    outputs = []
    for layer in range(2):
        params = smalls[layer]
        x_all, a, oqkv, lse, own, *away = call(
            functools.partial(attn_fwd_body, tensor, layer),
            [
                Kept((tokens, width), BF16),
                Kept((tokens, width), BF16),
                Kept((tokens, 4 * head_cols), BF16),
                Kept((tokens, 128), F32),
                *blocks,
            ],
            "attn_fwd", 2 * unit, [*xs, params, mask, attn_w],
            [vmem] * (tensor + 2) + [hbm], attn_room,
        )
        h, c = call(
            functools.partial(middle_body, tensor),
            [Kept((rows, width), F32), struct((rows, width), BF16)],
            "middle", 0, [xs[0], own, *to_tensor(away), params],
        )
        late = layer == 1
        c_all, m, der, own, *away = call(
            functools.partial(mlp_fwd_body, tensor),
            [
                Kept((tokens, width), BF16),
                Kept((tokens, hidden), BF16),
                Kept((tokens, hidden), F32),
                *(late_blocks if late else blocks),
            ],
            "mlp_fwd", 2 * unit, [*everywhere(c), params, mlp_w[layer]],
            [vmem] * (tensor + 1) + [hbm], mlp_room,
        )
        saved.append((xs[0], x_all, a, oqkv, lse, h, c_all, m, der))
        if late:
            carried = (own, away)
            continue
        (y,) = call(
            functools.partial(end_body, tensor),
            [struct((rows, width), BF16)],
            "end", 0, [Far(h), own, *to_tensor(away), params],
        )
        outputs.append(y)
        xs = everywhere(y)

    swap = lambda v: lax.ppermute(v, "section", [(0, 1), (1, 0)])

    def joined_halves(pairs, passing, after=()):
        keeps, sends = [p[0] for p in pairs], [swap(p[1]) for p in pairs]
        rows_each = sum(k.shape[1] for k in keeps)
        return call(
            functools.partial(join_body, dp),
            [struct((dp, rows_each, hidden), BF16), struct(passing.shape, passing.dtype)],
            "join", 0, [keeps[0], *map(distant, keeps[1:]), *sends, passing], after=after,
        )

    def over_dp(joined):
        joined = joined.reshape(-1, hidden)
        return lax.psum_scatter(joined, "dp", scatter_dimension=0, tiled=True)

    input_grads = [None] * 2
    pairs = []
    extra = []
    share = piece // tensor
    e, es = cots[0], cots
    for layer in (1, 0):
        params = smalls[layer]
        x, x_all, a, oqkv, lse, h, c_all, m, der = saved[layer]
        e_all, du, hidden_sum, own, *away = call(
            functools.partial(mlp_bwd_body, tensor),
            [
                Kept((tokens, width), BF16),
                Kept((tokens, hidden), BF16),
                struct((1, hidden), F32),
                *blocks,
            ],
            "mlp_bwd", 2 * unit, [*es, Far(der), mlp_w[layer]],
            [vmem] * (tensor + 1) + [hbm], mlp_room, extra,
        )
        received = to_tensor(away)
        mlp_grads = functools.partial(
            call,
            functools.partial(mlp_grads_body, dp),
            [struct((dp, 2 * half, hidden), BF16)] * 2,
            "mlp_grads", 2 * unit, [meta, Far(c_all), Far(e_all), Far(du), Far(m)],
            [smem] + [vmem] * 4, [pltpu.VMEM((2, width, hidden), F32)],
        )
        mlp_pair = mlp_grads(received)
        dh, dh_low, sums_mid = call(
            functools.partial(middle_back_body, tensor),
            [Kept((rows, width), F32), struct((rows, width), BF16), Kept((4, width), F32)],
            "middle_back", 0, [e, Far(h), own, *received, params],
            after=[mlp_pair[0]],
        )
        if layer == 1:
            joined, dh_low = joined_halves([mlp_pair], dh_low)
            mlp_1 = over_dp(joined)
        else:
            joined, dh_low = joined_halves([mlp_pair, *pairs], dh_low, [distant(mlp_1)])
            mix = over_dp(joined)
        dhs = everywhere(dh_low)
        dh_all, dqkv, qv_sums, own, *away = call(
            functools.partial(attn_bwd_body, tensor, layer),
            [
                Kept((tokens, width), BF16),
                Kept((tokens, 4 * head_cols), BF16),
                struct((2, head_cols), F32),
                blocks[0],
                *[struct((rows if layer == 1 else 2 * rows, width), BF16)] * (tensor - 1),
            ],
            "attn_bwd", 2 * unit,
            [*dhs, attn_w, Far(oqkv), Far(lse), mask, *(() if layer == 1 else map(Far, carried[1]))],
            [vmem] * tensor + [hbm] + [vmem] * (3 if layer == 1 else tensor + 2),
            attn_room,
        )
        received = to_tensor(away)
        whole = direct and layer == 0
        attn_grads = functools.partial(
            call,
            functools.partial(attn_grads_body, layer, dp),
            [struct((dp, piece + 16, 4 * head_cols), BF16)]
            if whole
            else [struct((dp, half + 16, 4 * head_cols), BF16)] * 2,
            "attn_grads", 3 * unit,
            [
                meta, Far(x_all), Far(dh_all), Far(a), Far(oqkv), Far(dqkv), attn_w,
                distant(sums_mid), hidden_sum, qv_sums,
            ],
            [smem] + [vmem] * 5 + [hbm] + [vmem] * 3,
            [pltpu.VMEM((width, 4 * head_cols), F32), *attn_room],
        )
        if layer == 1:
            pass
        elif direct:
            (grad,) = attn_grads()
            attn_own, *attn_away = call(
                split_body,
                [struct((piece + 16, hidden), F32)]
                + [struct((piece + 16, hidden), BF16)] * (dp - 1),
                "split", 0, [meta, grad, to_other(grad, 1)], [smem, vmem, vmem],
            )
            attn_others = to_dp(attn_away, 0)
        else:
            attn_0 = over_dp(joined_halves([attn_grads()], dh_low)[0])
            there = swap(attn_0)
            attn_own = jnp.concatenate(
                [jnp.where(layer_first, v[:half], w[:half]) for v, w in ((attn_0, there), (there, attn_0))]
                + [attn_0[half:]]
            ).astype(F32)
            attn_others = []
        if layer == 1:
            e, e_low = call(
                functools.partial(end_back_body, tensor),
                [struct((rows, width), F32), struct((rows, width), BF16)],
                "end_back", 0, [Far(dh), x, own, *received, params],
            )
            es = everywhere(e_low)
            attn_pair = attn_grads(es[1:2])
            pairs.append(attn_pair)
            extra = [attn_pair[0]]
        else:
            (sent,) = call(
                turn_body, [struct((3 * half, hidden), BF16)], "turn", 0, [meta, mlp_1, mix],
                [smem, vmem, vmem],
            )
            total, row_own, *row_away = call(
                functools.partial(small_body, len(attn_others)),
                [struct((16, width), F32)] + [struct((6, share), F32)] * tensor,
                "small", 0, [meta, mix, attn_own, *attn_others],
                [smem] + [vmem] * (2 + len(attn_others)),
            )
            e, y = call(
                functools.partial(last_body, tensor),
                [struct((rows, width), F32), struct((rows, width), BF16)],
                "last", 0,
                [Far(dh), x, own, *received, params, Far(saved[1][5]), Far(carried[0]), smalls[1]],
                after=[total],
            )
            outputs.append(y)
        input_grads[layer] = e

    pick = lambda pair: jnp.where(layer_first, pair[0], pair[1])
    flip = lambda pair: jnp.where(layer_first, pair[1], pair[0])
    def both(pair):
        here, there = pick(pair), swap(flip(pair))
        return jnp.stack([jnp.where(layer_first, here, there), jnp.where(layer_first, there, here)])[None, None]

    block_out = both(outputs)
    grads_out = both(input_grads)
    received = swap(sent)
    row_away = to_tensor(row_away)
    qv_cols = head_cols // dp
    qv_grad = lax.dynamic_slice(
        total, (7, d * qv_cols), (2, qv_cols), allow_negative_indices=False
    )
    w_qkv_grad, w_out_grad, w_fc1_grad, w_fc2_grad = call(
        functools.partial(finish_body, len(attn_others)),
        [
            struct((3, piece, head_cols), F32),
            struct((head_cols, piece), F32),
            struct((piece, hidden), F32),
            struct((piece, hidden), F32),
        ],
        "finish", 0, [meta, mlp_1, mix, received, attn_own, *attn_others],
        [smem] + [vmem] * (4 + len(attn_others)),
        [pltpu.VMEM((piece, 4 * head_cols), F32)],
    )
    (row_grad,) = call(
        rows_body, [struct((6, share), F32)], "rows", 0, [row_own, *row_away], after=[w_fc1_grad]
    )
    return (
        block_out,
        grads_out,
        row_grad[None],
        qv_grad.reshape(1, 2, 1, qv_cols),
        w_qkv_grad[None],
        w_out_grad[None],
        total[6:7, :piece][None],
        w_fc1_grad[None],
        w_fc2_grad.T[None],
    )


def solution(mesh):
    sizes = tuple(mesh.shape[axis] for axis in ("section", "dp", "tensor"))
    placed = (
        P("dp", None, "tensor", None),
        P("dp", None, "tensor", None),
        P("dp", None, None),
        P("section", None, "dp"),
        P("section", None, "tensor", "dp"),
        P("section", None, "dp", "tensor"),
        P("section", "tensor", "dp"),
        P("section", "tensor", "dp"),
        P("section", "dp", "tensor"),
        P("section", "tensor", "dp"),
    )
    return jax.shard_map(
        functools.partial(shards, sizes),
        mesh=mesh,
        in_specs=placed,
        out_specs=(
            P("section", "dp", None, "tensor", None),
            P("section", "dp", None, "tensor", None),
            P("section", None, ("dp", "tensor")),
            P("section", None, "tensor", "dp"),
            P("section", None, "dp", "tensor"),
            P("section", "tensor", "dp"),
            P("section", "tensor", "dp"),
            P("section", "dp", "tensor"),
            P("section", "tensor", "dp"),
        ),
        check_vma=False,
    )
```
